256 devices in a mesh: tok: 4 (over z_lo), kin: 8 (over x, core), nout: 8 (over y, z_hi).
Axes of the slice: x: 4, y: 4, z: 8 (z_hi: 2, z_lo: 4; z = z_hi * 4 + z_lo), core: 2. Of those that a mesh axis runs over, the one named last changes fastest.
Arguments:
- scan_out: bfloat16 [256, 16384], P('nout', ('tok', 'kin')), may hold values from -134 to 134
- gate_in: bfloat16 [256, 16384], P('nout', ('tok', 'kin')), may hold values from -6 to 6
- norm_gain: float32 [16384], P(('tok', 'kin')), may hold values from 0.25 to 1.75
- w_out: bfloat16 [16384, 8192], P(('tok', 'kin'), 'nout'), may hold values from -0.046875 to 0.046875
- resid: bfloat16 [256, 8192], P(('tok', 'kin'), 'nout'), may hold values from -48 to 48
- mlp_gain: float32 [8192], P('nout'), may hold values from 0.25 to 1.75
- w_up: bfloat16 [8192, 32768], P('nout', ('tok', 'kin')), may hold values from -0.0625 to 0.0625
- w_down: bfloat16 [32768, 8192], P(('tok', 'kin'), 'nout'), may hold values from -0.03125 to 0.03125
- cotangent: bfloat16 [256, 8192], P(('tok', 'kin'), 'nout'), may hold values from -21 to 21
Outputs:
- block_out: bfloat16 [256, 8192], P(('tok', 'kin'), 'nout')
- grad_scan: bfloat16 [256, 16384], P('nout', ('tok', 'kin'))
- grad_gate: bfloat16 [256, 16384], P('nout', ('tok', 'kin'))
- grad_norm_gain: float32 [16384], P(('tok', 'kin'))
- grad_w_out: bfloat16 [16384, 8192], P(('tok', 'kin'), 'nout')
- grad_resid: bfloat16 [256, 8192], P(('tok', 'kin'), 'nout')
- grad_mlp_gain: float32 [8192], P('nout')
- grad_w_up: bfloat16 [8192, 32768], P('nout', ('tok', 'kin'))
- grad_w_down: bfloat16 [32768, 8192], P(('tok', 'kin'), 'nout')
The draws below stay inside these ranges and needn't reach their ends.
All inputs are finite; a program needn't handle non-finite values.
Results may differ from the reference program's by a relative error of at most 0.01.
Values may be sent and summed in bfloat16 or wider, within the bound.
No kernel may reach another device: no remote copies, remote signals or barrier semaphores. Data moves between devices by JAX's collectives and lax.ppermute only.
A program may use at most 64 MiB of HBM per device.

```python
import math
import jax
import jax.numpy as jnp
from jax import lax

D = 8192
INNER = 16384
GROUPS = 8
FFN = 32768
TOKENS = 256


def draw_scan_out(key, part):
    key = jax.random.fold_in(key, 11)
    first, second, third = jax.random.split(key, 3)
    row_scale = jnp.exp(jax.random.uniform(first, (TOKENS, 1), jnp.float32) * math.log(10.0))
    col_scale = jnp.exp(jax.random.uniform(second, (1, INNER), jnp.float32) * math.log(10.0))
    base = jax.random.truncated_normal(third, -4.0, 4.0, (TOKENS, INNER), jnp.float32)
    return (base * row_scale * col_scale / 3.0).astype(jnp.bfloat16)


def draw_resid(key, part):
    key = jax.random.fold_in(key, 23)
    first, second, third = jax.random.split(key, 3)
    row_scale = jnp.exp(jax.random.uniform(first, (TOKENS, 1), jnp.float32, math.log(0.3), math.log(3.0)))
    col_scale = jnp.exp(jax.random.uniform(second, (1, D), jnp.float32, math.log(0.4), math.log(4.0)))
    base = jax.random.truncated_normal(third, -4.0, 4.0, (TOKENS, D), jnp.float32)
    return (base * row_scale * col_scale).astype(jnp.bfloat16)


def draw_cotangent(key, part):
    key = jax.random.fold_in(key, 37)
    first = jax.random.fold_in(key, 0)
    position = jnp.arange(TOKENS, dtype=jnp.float32)[:, None] / max(TOKENS - 1, 1)
    rising = jnp.exp(position * math.log(3.0))
    base = jax.random.truncated_normal(first, -4.0, 4.0, (TOKENS, D), jnp.float32)
    return (base * rising).astype(jnp.bfloat16)


def level_of(rng, extent, cuts, low, high):
    factor_of, own = 1.0, jax.random.fold_in(rng, 6)
    for axis_at, parts in cuts:
        steps = jnp.exp(jax.random.uniform(jax.random.fold_in(own, axis_at), (parts,), jnp.float32, low / len(cuts), high / len(cuts)))
        factor_of = factor_of * jnp.repeat(steps, extent[axis_at] // parts).reshape([-1 if axis == axis_at else 1 for axis in range(len(extent))])
    return factor_of


def normal_values(stream_key, dims, width, bound, cuts=(), kind=jnp.bfloat16):
    array = jax.random.normal(stream_key, dims, jnp.float32) * width
    if len(cuts) > 0:
        array = level_of(stream_key, dims, cuts, -0.22, 0.18) * array
    return jnp.clip(array, min=-bound, max=bound).astype(kind)


def setup_inputs(seed: int = 0) -> dict:
    key_list = jax.random.split(jax.random.key(seed), 10)
    scan_out = draw_scan_out(jax.random.fold_in(key_list[9], 71), 0)
    gate_in = normal_values(key_list[1], (TOKENS, INNER), 1.5, 6.0, ((0, 8), (1, 32)))
    norm_gain = jnp.clip(1.0 + 0.15 * jax.random.normal(key_list[2], (INNER,), jnp.float32), 0.25, 1.75)
    w_out = normal_values(key_list[3], (INNER, D), INNER ** -0.5, 0.046875, ((0, 32), (1, 8)))
    resid = draw_resid(jax.random.fold_in(key_list[9], 71), 0)
    mlp_gain = jnp.clip(1.0 + 0.15 * jax.random.normal(key_list[5], (D,), jnp.float32), 0.25, 1.75)
    w_up = normal_values(key_list[6], (D, FFN), D ** -0.5, 0.0625, ((0, 8), (1, 32)))
    w_down = normal_values(key_list[7], (FFN, D), FFN ** -0.5, 0.03125, ((0, 32), (1, 8)))
    cotangent = draw_cotangent(jax.random.fold_in(key_list[9], 71), 0)
    return {"scan_out": scan_out, "gate_in": gate_in, "norm_gain": norm_gain, "w_out": w_out, "resid": resid, "mlp_gain": mlp_gain, "w_up": w_up, "w_down": w_down, "cotangent": cotangent}


epsilon = 1e-05

def reference(scan_out, gate_in, norm_gain, w_out, resid, mlp_gain, w_up, w_down, cotangent):
    scan_float = scan_out.astype(jnp.float32)
    gate_float = gate_in.astype(jnp.float32)
    logistic = jax.nn.sigmoid(gate_float)
    gated_unit = gate_float * logistic
    product = scan_float * gated_unit
    grouped = product.reshape(TOKENS, GROUPS, INNER // GROUPS)
    scale_rows = lax.rsqrt(lax.optimization_barrier(jnp.mean(grouped * grouped, axis=-1, keepdims=True)) + epsilon)
    normed_group = grouped * scale_rows
    normed = normed_group.reshape(TOKENS, INNER)
    mixed_rows = (normed * norm_gain[None, :]).astype(jnp.bfloat16)
    projected = jnp.dot(mixed_rows, w_out, preferred_element_type=jnp.float32)
    stream = lax.optimization_barrier((resid.astype(jnp.float32) + projected).astype(jnp.bfloat16))
    stream_float = stream.astype(jnp.float32)
    stream_scale = lax.rsqrt(lax.optimization_barrier(jnp.mean(stream_float * stream_float, axis=-1, keepdims=True)) + epsilon)
    unit_rows = stream_float * stream_scale
    up_input = (unit_rows * mlp_gain[None, :]).astype(jnp.bfloat16)
    hidden_pre = jnp.dot(up_input, w_up, preferred_element_type=jnp.float32)
    squared = jnp.square(jax.nn.relu(hidden_pre)).astype(jnp.bfloat16)
    down_out = jnp.dot(squared, w_down, preferred_element_type=jnp.float32)
    block_out = (stream_float + down_out).astype(jnp.bfloat16)
    grad_w_down = jnp.dot(squared.T, cotangent, preferred_element_type=jnp.float32).astype(jnp.bfloat16)
    hidden_back = jnp.dot(cotangent, w_down.T, preferred_element_type=jnp.float32)
    hidden_delta = (2.0 * jax.nn.relu(hidden_pre) * hidden_back).astype(jnp.bfloat16)
    grad_w_up = jnp.dot(up_input.T, hidden_delta, preferred_element_type=jnp.float32).astype(jnp.bfloat16)
    up_back = jnp.dot(hidden_delta, w_up.T, preferred_element_type=jnp.float32)
    grad_mlp_gain = lax.optimization_barrier(jnp.sum(up_back * unit_rows, axis=0))
    unit_back = up_back * mlp_gain[None, :]
    inner_rows = lax.optimization_barrier(jnp.mean(unit_back * unit_rows, axis=-1, keepdims=True))
    grad_resid = (cotangent.astype(jnp.float32) + stream_scale * (unit_back - unit_rows * inner_rows)).astype(jnp.bfloat16)
    grad_w_out = jnp.dot(mixed_rows.T, grad_resid, preferred_element_type=jnp.float32).astype(jnp.bfloat16)
    mixed_back = jnp.dot(grad_resid, w_out.T, preferred_element_type=jnp.float32)
    grad_norm_gain = lax.optimization_barrier(jnp.sum(mixed_back * normed, axis=0))
    normed_grad = (mixed_back * norm_gain[None, :]).reshape(TOKENS, GROUPS, INNER // GROUPS)
    group_dots = lax.optimization_barrier(jnp.mean(normed_grad * normed_group, axis=-1, keepdims=True))
    product_back = (scale_rows * (normed_grad - normed_group * group_dots)).reshape(TOKENS, INNER)
    grad_scan = (product_back * gated_unit).astype(jnp.bfloat16)
    grad_gate = (product_back * scan_float * logistic * (1.0 + gate_float * (1.0 - logistic))).astype(jnp.bfloat16)
    return (block_out, grad_scan, grad_gate, grad_norm_gain, grad_w_out, grad_resid, grad_mlp_gain, grad_w_up, grad_w_down)
```

```python
import jax
import jax.numpy as jnp
from jax import lax
from jax.sharding import Mesh, PartitionSpec as P

D = 8192
INNER = 16384
GROUPS = 8
AUX = 128

epsilon = 1e-05
f32 = jnp.float32
bf16 = jnp.bfloat16


def swapped(value, axis, mask):
    return lax.ppermute(value, axis, [(i, i ^ mask) for i in range(lax.axis_size(axis))])


def around(value, axis):
    return [value] + [swapped(value, axis, mask) for mask in (1, 2, 3)]


def placed(parts, index, axis):
    bit = 1
    while bit < len(parts):
        flip = (index & bit) != 0
        parts = [jnp.where(flip, parts[j ^ bit], parts[j]) for j in range(len(parts))]
        bit *= 2
    return jnp.stack(parts, axis)


def pick(value, index, axis):
    return lax.dynamic_index_in_dim(value, index, axis, keepdims=False)


def total(parts):
    first, second, third, fourth = [part.astype(f32) for part in parts]
    return (first + second) + (third + fourth)


def halves(value):
    high = lax.reduce_precision(value, 8, 7)
    return high, value - high


def columns(*values):
    rows = values[0].shape
    spot = lax.broadcasted_iota(jnp.int32, rows + (AUX,), len(rows))
    block = jnp.zeros(rows + (AUX,), f32)
    for k, value in enumerate(values):
        high, low = halves(value)
        block = jnp.where(spot == 2 * k, high[..., None], block)
        block = jnp.where(spot == 2 * k + 1, low[..., None], block)
    return block


def column(block, k):
    return block[..., 2 * k].astype(f32) + block[..., 2 * k + 1].astype(f32)


def lines(value, width):
    high, low = halves(value)
    block = jnp.concatenate([high[None], low[None], jnp.zeros((14,) + value.shape, f32)])
    if width > value.shape[0]:
        block = jnp.pad(block, ((0, 0), (0, width - value.shape[0])))
    return block.astype(bf16)


def line(block):
    return block[0].astype(f32) + block[1].astype(f32)


def contract_rows(left, right):
    return lax.dot_general(left, right, (((0,), (0,)), ((), ())), preferred_element_type=f32)


def contract_cols(left, right):
    return lax.dot_general(left, right, (((1,), (1,)), ((), ())), preferred_element_type=f32)


def shards(scan_out, gate_in, norm_gain, w_out, resid, mlp_gain, w_up, w_down, cotangent):
    it, ix, ic = lax.axis_index("tok"), lax.axis_index("x"), lax.axis_index("core")
    iy, iz = lax.axis_index("y"), lax.axis_index("zh")
    group_width = INNER // GROUPS

    scan_float = scan_out.astype(f32)
    gate_float = gate_in.astype(f32)
    logistic = jax.nn.sigmoid(gate_float)
    gated_unit = gate_float * logistic
    product = scan_float * gated_unit
    totals = jnp.sum(product * product, axis=1)
    totals = totals + swapped(totals, "core", 1)
    totals = totals + swapped(totals, "x", 1)
    scale_rows = lax.rsqrt(totals / group_width + epsilon)
    normed = product * scale_rows[:, None]
    mixed_rows = (normed * norm_gain[None, :]).astype(bf16)
    mixed = placed([mixed_rows, swapped(mixed_rows, "zh", 1)], iz, 0).reshape(64, -1)
    mixed = placed(around(mixed, "y"), iy, 0).reshape(256, -1)

    both = jnp.concatenate([cotangent, resid], axis=0)
    both = placed(around(both, "tok"), it, 0)
    cot_tok, resid_tok = both[:, :8], both[:, 8:]
    cot = placed(around(cot_tok, "x"), ix, 1)
    cot = placed([cot, swapped(cot, "core", 1)], ic, 2).reshape(256, -1)

    partial = jnp.dot(mixed, w_out, preferred_element_type=f32).reshape(16, 2, 8, -1)
    summed = pick(partial, ic, 1) + swapped(pick(partial, 1 - ic, 1), "core", 1)
    summed = summed.reshape(4, 4, 8, -1)
    summed = total(
        [pick(summed, ix, 1)]
        + [swapped(pick(summed, ix ^ d, 1).astype(bf16), "x", d) for d in (1, 2, 3)]
    )
    summed = total(around(summed.astype(bf16), "tok"))
    stream = lax.reduce_precision(resid_tok.astype(f32) + summed, 8, 7)
    rows = stream.astype(bf16)
    rows = placed(around(rows, "x"), ix, 1)
    rows = placed([rows, swapped(rows, "core", 1)], ic, 2).reshape(256, -1)

    rows_float = rows.astype(f32)
    squares = jnp.sum(rows_float * rows_float, axis=1)
    raw = jnp.dot((rows_float * mlp_gain[None, :]).astype(bf16), w_up, preferred_element_type=f32)
    back = contract_cols(cot, w_down)
    width = raw.shape[1]
    wide = jnp.concatenate([raw, back, columns(squares)], axis=1).reshape(4, 64, -1)
    wide = total(
        [pick(wide, iy, 0)]
        + [swapped(pick(wide, iy ^ d, 0).astype(bf16), "y", d) for d in (1, 2, 3)]
    )
    squares = column(wide[:, 2 * width :], 0)
    other = swapped(
        jnp.concatenate([wide[:, : 2 * width], columns(squares)], axis=1).astype(bf16), "zh", 1
    )
    squares = squares + column(other[:, 2 * width :], 0)
    stream_scale = lax.rsqrt(squares / D + epsilon)
    pre = (wide[:, :width] + other[:, :width].astype(f32)) * stream_scale[:, None]
    back = wide[:, width : 2 * width] + other[:, width : 2 * width].astype(f32)
    active = jax.nn.relu(pre)
    squared = jnp.square(active)
    delta = 2.0 * active * back
    inner = jnp.sum(delta * pre, axis=1)
    hidden = jnp.concatenate([squared, delta, columns(stream_scale, inner)], axis=1).astype(bf16)
    hidden = placed(around(hidden, "y"), iy, 0).reshape(256, -1)
    squared, delta, extra = hidden[:, :width], hidden[:, width : 2 * width], hidden[:, 2 * width :]
    scales, inner = column(extra, 0), column(extra, 1)

    up_back = contract_cols(delta, w_up)
    down = jnp.dot(squared, w_down, preferred_element_type=f32)
    feats = up_back.shape[1]
    wide = jnp.concatenate([up_back, down, columns(inner)], axis=1).reshape(16, 2, 8, -1)
    wide = pick(wide, ic, 1) + swapped(pick(wide, 1 - ic, 1).astype(bf16), "core", 1).astype(f32)
    wide = wide.reshape(4, 4, 8, -1)
    wide = total(
        [pick(wide, ix, 1)]
        + [swapped(pick(wide, ix ^ d, 1).astype(bf16), "x", d) for d in (1, 2, 3)]
    )
    inner = column(wide[..., 2 * feats :], 0)
    down = wide[..., feats : 2 * feats]
    mine = jnp.concatenate([wide[..., :feats], columns(inner)], axis=-1).astype(bf16)
    mine = mine.reshape(32, -1)
    pad = ((0, 0), (0, AUX))
    parts = [
        swapped(jnp.concatenate([mine, jnp.pad(pick(down, it ^ d, 0).astype(bf16), pad)]), "tok", d)
        for d in (1, 2, 3)
    ]
    down = total([pick(down, it, 0)] + [part[32:, :feats] for part in parts])
    block_out = (pick(stream, it, 0) + down).astype(bf16)
    summed = total([mine] + [part[:32] for part in parts]).reshape(4, 8, -1)
    up_back, inner = summed[..., :feats], column(summed[..., feats:], 0)
    own_scale = pick(pick(scales.reshape(4, 4, 2, 8), ix, 1), ic, 1)[..., None]
    unit = stream * own_scale
    unit_back = up_back * mlp_gain
    grad_tok = (
        cot_tok.astype(f32) + own_scale * (unit_back - unit * (inner / D)[..., None])
    ).astype(bf16)
    grad_resid = pick(grad_tok, it, 0)
    gain_sum = jnp.sum(up_back * unit, axis=(0, 1))
    parts = around(jnp.concatenate([grad_tok.reshape(32, -1), lines(gain_sum, feats)]), "x")
    gain_sum = lines(total([line(part[32:]) for part in parts]), feats)
    grads = placed([part[:32].reshape(4, 8, -1) for part in parts], ix, 1)
    other = swapped(jnp.concatenate([grads.reshape(128, -1), gain_sum]), "core", 1)
    grad_mlp_gain = line(gain_sum) + line(other[128:])
    grads = placed([grads, other[:128].reshape(4, 4, 8, -1)], ic, 2).reshape(256, -1)

    mixed_back = contract_cols(grads, w_out)
    dots = mixed_back * mixed.astype(f32)
    gain_sum = jnp.sum(dots, axis=0)
    dots = jnp.sum(dots, axis=1)
    units = mixed_back.shape[1]
    wide = jnp.concatenate([mixed_back, columns(dots)], axis=1).reshape(4, 64, -1)
    gain_sum = lines(gain_sum, units + AUX)
    parts = [
        swapped(jnp.concatenate([pick(wide, iy ^ d, 0).astype(bf16), gain_sum]), "y", d)
        for d in (1, 2, 3)
    ]
    wide = total([pick(wide, iy, 0)] + [part[:64] for part in parts])
    gain_sum = total([line(gain_sum)] + [line(part[64:]) for part in parts])
    gain_sum = lines(gain_sum[:units], units + AUX)
    dots = column(wide[:, units:], 0)
    mixed_back = pick(wide[:, :units].reshape(2, 32, -1), iz, 0)
    sent = pick(wide[:, :units].reshape(2, 32, -1), 1 - iz, 0)
    sent = jnp.concatenate([sent, columns(pick(dots.reshape(2, 32), 1 - iz, 0))], axis=1).astype(bf16)
    other = swapped(jnp.concatenate([sent, gain_sum]), "zh", 1)
    mixed_back = mixed_back + other[:32, :units].astype(f32)
    dots = pick(dots.reshape(2, 32), iz, 0) + column(other[:32, units:], 0)
    grad_norm_gain = (line(gain_sum) + line(other[32:]))[:units] / norm_gain
    dots = dots + swapped(dots, "core", 1)
    dots = dots + swapped(dots, "x", 1)
    product_back = scale_rows[:, None] * (
        mixed_back * norm_gain[None, :] - normed * (dots / group_width)[:, None]
    )
    grad_scan = (product_back * gated_unit).astype(bf16)
    grad_gate = (
        product_back * scan_float * logistic * (1.0 + gate_float * (1.0 - logistic))
    ).astype(bf16)

    grad_w_down = contract_rows(squared, cot).astype(bf16)
    up_in = (rows_float * scales[:, None] * mlp_gain[None, :]).astype(bf16)
    grad_w_up = contract_rows(up_in, delta).astype(bf16)
    grad_w_out = contract_rows(mixed, grads).astype(bf16)
    return (
        block_out,
        grad_scan,
        grad_gate,
        grad_norm_gain,
        grad_w_out,
        grad_resid,
        grad_mlp_gain,
        grad_w_up,
        grad_w_down,
    )


def solution(mesh):
    fine = Mesh(mesh.devices.reshape(4, 4, 2, 4, 2), ("tok", "x", "core", "y", "zh"))
    tk, nout = ("tok", "x", "core"), ("y", "zh")
    in_specs = (
        P(nout, tk),
        P(nout, tk),
        P(tk),
        P(tk, nout),
        P(tk, nout),
        P(nout),
        P(nout, tk),
        P(tk, nout),
        P(tk, nout),
    )
    out_specs = (
        P(tk, nout),
        P(nout, tk),
        P(nout, tk),
        P(tk),
        P(tk, nout),
        P(tk, nout),
        P(nout),
        P(nout, tk),
        P(tk, nout),
    )
    return jax.shard_map(shards, mesh=fine, in_specs=in_specs, out_specs=out_specs, check_vma=False)
```

```python
import jax
import jax.numpy as jnp
from jax import lax
from jax.experimental.layout import Layout, with_layout_constraint
from jax.sharding import Mesh, PartitionSpec as P

D = 8192
INNER = 16384
GROUPS = 8
AUX = 128

epsilon = 1e-05
f32 = jnp.float32
bf16 = jnp.bfloat16


def rowed(value):
    return with_layout_constraint(value, Layout(major_to_minor=tuple(range(value.ndim))))


def swapped(value, axis, mask):
    pairs = [(i, i ^ mask) for i in range(lax.axis_size(axis))]
    return rowed(lax.ppermute(rowed(value), axis, pairs))


def sent(pieces, axis):
    second, third, first = [swapped(pieces[d], axis, d) for d in (2, 3, 1)]
    return [first, second, third]


def around(value, axis):
    return [value] + sent([value] * 4, axis)


def placed(parts, index):
    bit = 1
    while bit < len(parts):
        flip = (index & bit) != 0
        parts = [jnp.where(flip, parts[j ^ bit], parts[j]) for j in range(len(parts))]
        bit *= 2
    return jnp.concatenate(parts)


def total(parts):
    first, second, third, fourth = [part.astype(f32) for part in parts]
    return (first + second) + (third + fourth)


def halves(value):
    high = lax.reduce_precision(value, 8, 7)
    return high, value - high


def columns(*values):
    rows = values[0].shape[0]
    spot = lax.broadcasted_iota(jnp.int32, (rows, AUX), 1)
    block = jnp.zeros((rows, AUX), f32)
    for k, value in enumerate(values):
        high, low = halves(value)
        block = jnp.where(spot == 2 * k, high, block)
        block = jnp.where(spot == 2 * k + 1, low, block)
    return block.astype(bf16)


def column(block, k):
    return block[:, 2 * k : 2 * k + 1].astype(f32) + block[:, 2 * k + 1 : 2 * k + 2].astype(f32)


def lines(value, width):
    high, low = halves(value)
    spot = lax.broadcasted_iota(jnp.int32, (16, value.shape[1]), 0)
    block = jnp.where(spot == 0, high, jnp.where(spot == 1, low, 0.0)).astype(bf16)
    return jnp.pad(block, ((0, 0), (0, width - value.shape[1])))


def line(block):
    return block[0:1].astype(f32) + block[1:2].astype(f32)


def either(block):
    rows = lax.broadcasted_iota(jnp.int32, (block.shape[0], 1), 0)
    return jnp.where((rows & 64) == 0, column(block, 0), column(block, 1))


def turned(value, mask):
    return jnp.concatenate([value[8 * (j ^ mask) : 8 * (j ^ mask) + 8] for j in range(4)])


def contract_rows(left, right):
    return lax.dot_general(left, right, (((0,), (0,)), ((), ())), preferred_element_type=f32)


def contract_cols(left, right):
    return lax.dot_general(left, right, (((1,), (1,)), ((), ())), preferred_element_type=f32)


def shards(scan_out, gate_in, norm_gain, w_out, resid, mlp_gain, w_up, w_down, cotangent):
    it, ix, ic = lax.axis_index("tok"), lax.axis_index("x"), lax.axis_index("core")
    iy, iz = lax.axis_index("y"), lax.axis_index("zh")
    group_width = INNER // GROUPS
    units, feats = w_out.shape
    cat = jnp.concatenate

    def one_hot(at_home, at_norm):
        home = (
            ((it ^ ((at_home >> 3) & 3)) << 6)
            | ((ix ^ ((at_home >> 5) & 3)) << 4)
            | ((ic ^ (at_home >> 7)) << 3)
            | (at_home & 7)
        )
        norm = ((iy ^ (at_norm >> 6)) << 6) | ((iz ^ ((at_norm >> 5) & 1)) << 5) | (at_norm & 31)
        return (home == norm).astype(bf16)

    across = lax.broadcasted_iota(jnp.int32, (256, 256), 1)
    along = lax.broadcasted_iota(jnp.int32, (256, 256), 0)
    to_home, to_norm = one_hot(along, across), one_hot(across, along)

    scan_float = scan_out.astype(f32)
    gate_float = gate_in.astype(f32)
    logistic = jax.nn.sigmoid(gate_float)
    gated_unit = gate_float * logistic
    product = scan_float * gated_unit
    squares = jnp.sum(product * product, axis=1, keepdims=True)
    rows = cat([(product * norm_gain[None, :]).astype(bf16), columns(squares)], axis=1)
    rows = cat([rows, swapped(rows, "zh", 1)])
    rows = cat(around(rows, "y"))
    rows = jnp.dot(to_home, rows, preferred_element_type=f32)
    squares = column(rows[:, units:], 0)
    product_all = rows[:, :units].astype(bf16)

    partial = jnp.dot(product_all[128:], w_out, preferred_element_type=f32)
    spot = lax.broadcasted_iota(jnp.int32, (128, AUX), 1)
    other = swapped(cat([partial, jnp.where(spot == 0, squares[128:], 0.0)], axis=1), "core", 1)
    partial = jnp.dot(product_all[:128], w_out, preferred_element_type=f32) + other[:, :feats]
    squares = squares[:128] + other[:, feats : feats + 1]
    packed = cat([partial.astype(bf16), columns(squares)], axis=1)
    parts = [packed] + sent([packed[32 * d : 32 * d + 32] for d in range(4)], "x")
    parts = [part[:32].astype(f32) for part in parts]
    near, far = parts[0] + parts[1], parts[2] + parts[3]
    scale_near = lax.rsqrt(column(near[:, feats:], 0) / group_width + epsilon)
    scale_far = lax.rsqrt(column(far[:, feats:], 0) / group_width + epsilon)
    near, far = near[:, :feats] * scale_near, far[:, :feats] * scale_far
    summed = near + far
    summed = cat([summed[:8] + resid.astype(f32), summed[8:]]).astype(bf16)
    parts = around(cat([summed, cotangent]), "tok")
    cot_tok = cat([part[32:] for part in parts])
    stream = lax.reduce_precision(total([turned(parts[d][:32], d) for d in range(4)]), 8, 7)
    parts = around(cat([stream.astype(bf16), cot_tok, columns(scale_near, scale_far)], axis=1), "x")
    rows = cat(parts)
    rows = cat([rows, swapped(rows, "core", 1)])
    rows, cot, group_scale = rows[:, :feats], rows[:, feats : 2 * feats], either(rows[:, 2 * feats :])
    mixed = (product_all.astype(f32) * group_scale).astype(bf16)

    def pieces(value):
        value = value.reshape(4, 64, -1)
        return [lax.dynamic_index_in_dim(value, iy ^ d, 0, keepdims=False) for d in range(4)]

    back = pieces(contract_cols(cot, w_down))
    back = total([back[0]] + sent([piece.astype(bf16) for piece in back], "y"))
    back = back + swapped(back.astype(bf16), "zh", 1).astype(f32)
    back = placed(around(back.astype(bf16), "y"), iy)

    rows_float = rows.astype(f32)
    squares = pieces(jnp.sum(rows_float * rows_float, axis=1, keepdims=True))
    raw = pieces(
        jnp.dot((rows_float * mlp_gain[None, :]).astype(bf16), w_up, preferred_element_type=f32)
    )
    width = raw[0].shape[1]
    parts = sent([cat([r.astype(bf16), columns(s)], axis=1) for r, s in zip(raw, squares)], "y")
    raw = total([cat([raw[0], columns(squares[0]).astype(f32)], axis=1)] + parts)
    raw, squares = raw[:, :width], column(raw[:, width:], 0)
    other = swapped(cat([raw.astype(bf16), columns(squares)], axis=1), "zh", 1)
    squares = squares + column(other[:, width:], 0)
    stream_scale = lax.rsqrt(squares / D + epsilon)
    pre = (raw + other[:, :width].astype(f32)) * stream_scale
    pre = placed(around(cat([pre.astype(bf16), columns(stream_scale)], axis=1), "y"), iy)
    scales = column(pre[:, width:], 0)
    active = jax.nn.relu(pre[:, :width].astype(f32))
    squared = jnp.square(active).astype(bf16)
    slope = 2.0 * active * back.astype(f32)
    delta = slope.astype(bf16)
    inner = jnp.sum(slope * active, axis=1, keepdims=True)

    def down_half(rows):
        return jnp.dot(rows, w_down, preferred_element_type=f32).astype(bf16)

    up_back = contract_cols(delta[128:], w_up).astype(bf16)
    inner = columns(inner)
    other = swapped(cat([up_back, down_half(squared[128:]), inner[128:]], axis=1), "core", 1)
    other = other.astype(f32)
    up_back = contract_cols(delta[:128], w_up) + other[:, :feats]
    down = other[:, feats : 2 * feats]
    inner = columns(column(inner[:128].astype(f32) + other[:, 2 * feats :], 0))
    packed = cat([up_back.astype(bf16), inner], axis=1)
    packed, squared = lax.optimization_barrier((packed, squared))
    parts = [packed[:32]] + sent([packed[32 * d : 32 * d + 32] for d in range(4)], "x")
    down = (down_half(squared[:128]).astype(f32) + down).astype(bf16)
    grad_w_down = contract_rows(squared, cot).astype(bf16)
    mine = total(parts)
    mine = cat([mine[:, :feats].astype(bf16), columns(column(mine[:, feats:], 0))], axis=1)
    mine, grad_w_down = lax.optimization_barrier((mine, grad_w_down))
    parts = around(mine, "tok")
    mine = total([turned(parts[d], d) for d in range(4)])
    up_back, inner = mine[:, :feats], column(mine[:, feats:], 0)
    own_scale = scales[:32]
    unit = stream * own_scale
    unit_back = up_back * mlp_gain[None, :]
    grads = lax.reduce_precision(
        cot_tok.astype(f32) + own_scale * (unit_back - unit * (inner / D)), 8, 7
    )
    grad_resid = grads[:8].astype(bf16)
    dot_near = jnp.sum(grads * near, axis=1, keepdims=True)
    dot_far = jnp.sum(grads * far, axis=1, keepdims=True)
    gain_sum = lines(jnp.sum(up_back * unit, axis=0, keepdims=True), feats + AUX)
    packed = cat([grads.astype(bf16), columns(dot_near, dot_far)], axis=1)
    packed = cat([packed, gain_sum])
    packed, delta = lax.optimization_barrier((packed, delta))
    parts = around(packed, "x")
    up_in = (rows_float * scales * mlp_gain[None, :]).astype(bf16)
    grad_w_up = contract_rows(up_in, delta).astype(bf16)
    gain_sum = lines(total([line(part[32:, :feats]) for part in parts]), feats + AUX)
    packed = cat([part[:32] for part in parts] + [gain_sum])
    packed, grad_w_up = lax.optimization_barrier((packed, grad_w_up))
    other = swapped(packed, "core", 1)
    grad_mlp_gain = (line(gain_sum) + line(other[128:]))[0, :feats]
    packed = cat([packed[:128], other[:128]])
    grads, dots = packed[:, :feats], either(packed[:, feats:])

    mixed_back = contract_cols(grads, w_out)
    gain_sum = jnp.sum(mixed_back * mixed.astype(f32), axis=0, keepdims=True)
    gain_sum = lines(gain_sum, units + AUX)
    rows = cat([mixed_back.astype(bf16), columns(dots, group_scale)], axis=1)
    rows = jnp.dot(to_norm, rows, preferred_element_type=f32).astype(bf16)
    group_scale = column(rows[:32, units:], 1)
    parts = [cat([rows[64 * d : 64 * d + 64], gain_sum]) for d in range(4)]
    parts, down = lax.optimization_barrier((parts, down))
    parts = parts[:1] + sent(parts, "y")
    down = [down[:32]] + sent([down[32 * d : 32 * d + 32] for d in range(4)], "x")
    down = total(down)
    summed = total(parts)
    mixed_back, gain_sum = summed[:64], lines(summed[64:65] + summed[65:66], units + AUX)
    dots = column(mixed_back[:, units:], 0)
    packed = cat([mixed_back[32:, :units].astype(bf16), columns(dots[32:])], axis=1)
    packed = cat([packed, gain_sum])
    packed, mixed, grads, down = lax.optimization_barrier((packed, mixed, grads, down))
    other = swapped(packed, "zh", 1)
    parts = [down[:8]] + sent([down[8 * d : 8 * d + 8].astype(bf16) for d in range(4)], "tok")
    block_out = (stream[:8] + total(parts)).astype(bf16)
    grad_w_out = contract_rows(mixed, grads).astype(bf16)
    mixed_back = mixed_back[:32, :units] + other[:32, :units].astype(f32)
    dots = dots[:32] + column(other[:32, units:], 0)
    grad_norm_gain = (line(gain_sum) + line(other[32:]))[0, :units] / norm_gain
    normed = product * group_scale
    product_back = group_scale * (mixed_back * norm_gain[None, :] - normed * (dots / group_width))
    grad_scan = (product_back * gated_unit).astype(bf16)
    grad_gate = (
        product_back * scan_float * logistic * (1.0 + gate_float * (1.0 - logistic))
    ).astype(bf16)
    return (
        block_out,
        grad_scan,
        grad_gate,
        grad_norm_gain,
        grad_w_out,
        grad_resid,
        grad_mlp_gain,
        grad_w_up,
        grad_w_down,
    )


def solution(mesh):
    fine = Mesh(mesh.devices.reshape(4, 4, 2, 4, 2), ("tok", "x", "core", "y", "zh"))
    tk, nout = ("tok", "x", "core"), ("y", "zh")
    in_specs = (
        P(nout, tk),
        P(nout, tk),
        P(tk),
        P(tk, nout),
        P(tk, nout),
        P(nout),
        P(nout, tk),
        P(tk, nout),
        P(tk, nout),
    )
    out_specs = (
        P(tk, nout),
        P(nout, tk),
        P(nout, tk),
        P(tk),
        P(tk, nout),
        P(tk, nout),
        P(nout),
        P(nout, tk),
        P(tk, nout),
    )
    return jax.shard_map(shards, mesh=fine, in_specs=in_specs, out_specs=out_specs, check_vma=False)
```

```python
import jax
import jax.numpy as jnp
from jax import lax
from jax.experimental import pallas as pl
from jax.experimental.layout import Layout, with_layout_constraint
from jax.experimental.pallas import tpu as pltpu
from jax.sharding import Mesh, PartitionSpec as P

D = 8192
INNER = 16384
GROUPS = 8
AUX = 128

epsilon = 1e-05
f32 = jnp.float32
bf16 = jnp.bfloat16


def rowed(value):
    return with_layout_constraint(value, Layout(major_to_minor=tuple(range(value.ndim))))


def swapped(value, axis, mask):
    pairs = [(i, i ^ mask) for i in range(lax.axis_size(axis))]
    return rowed(lax.ppermute(rowed(value), axis, pairs))


def sent(pieces, axis):
    second, third, first = [swapped(pieces[d], axis, d) for d in (2, 3, 1)]
    return [first, second, third]


def around(value, axis):
    return [value] + sent([value] * 4, axis)


def placed(parts, index):
    bit = 1
    while bit < len(parts):
        flip = (index & bit) != 0
        parts = [jnp.where(flip, parts[j ^ bit], parts[j]) for j in range(len(parts))]
        bit *= 2
    return jnp.concatenate(parts)


def total(parts):
    first, second, third, fourth = [part.astype(f32) for part in parts]
    return (first + second) + (third + fourth)


def halves(value):
    high = lax.reduce_precision(value, 8, 7)
    return high, value - high


def columns(*values):
    rows = values[0].shape[0]
    spot = lax.broadcasted_iota(jnp.int32, (rows, AUX), 1)
    block = jnp.zeros((rows, AUX), f32)
    for k, value in enumerate(values):
        high, low = halves(value)
        block = jnp.where(spot == 2 * k, high, block)
        block = jnp.where(spot == 2 * k + 1, low, block)
    return block.astype(bf16)


def column(block, k):
    return block[:, 2 * k : 2 * k + 1].astype(f32) + block[:, 2 * k + 1 : 2 * k + 2].astype(f32)


def lines(value, width):
    high, low = halves(value)
    spot = lax.broadcasted_iota(jnp.int32, (16, value.shape[1]), 0)
    block = jnp.where(spot == 0, high, jnp.where(spot == 1, low, 0.0)).astype(bf16)
    return jnp.pad(block, ((0, 0), (0, width - value.shape[1])))


def line(block):
    return block[0:1].astype(f32) + block[1:2].astype(f32)


def either(block):
    rows = lax.broadcasted_iota(jnp.int32, (block.shape[0], 1), 0)
    return jnp.where((rows & 64) == 0, column(block, 0), column(block, 1))


def turned(value, mask):
    return jnp.concatenate([value[8 * (j ^ mask) : 8 * (j ^ mask) + 8] for j in range(4)])


def contract_rows(left, right):
    return lax.dot_general(left, right, (((0,), (0,)), ((), ())), preferred_element_type=f32)


def contract_cols(left, right):
    return lax.dot_general(left, right, (((1,), (1,)), ((), ())), preferred_element_type=f32)


VMEM = pl.BlockSpec(memory_space=pltpu.VMEM)


def split(scratch, index, own, pieces):
    rows = own.shape[0]
    for d, piece in enumerate([own] + pieces):
        block = scratch[pl.ds(pl.multiple_of((index ^ d) * rows, rows), rows), :]
        piece[...] = block.astype(piece.dtype)


def both_halves(near, far, start, stop):
    return jnp.concatenate([near[:, start:stop], far[:, start:stop]])


def slope_kernel(index, near, far, weight, own, one, two, three, scratch):
    feats = weight.shape[1]
    cot = both_halves(near, far, feats, 2 * feats)
    scratch[...] = contract_cols(cot, weight[...])
    split(scratch, index[0], own, [one, two, three])


def raw_kernel(index, near, far, gain, weight, own, one, two, three, rows_out, cot_out, scratch):
    feats, width = weight.shape
    cot_out[...] = both_halves(near, far, feats, 2 * feats)
    rows = both_halves(near, far, 0, feats)
    rows_out[...] = rows
    rows = rows.astype(f32)
    squares = jnp.sum(rows * rows, axis=1, keepdims=True)
    high = squares.astype(bf16).astype(f32)
    spot = lax.broadcasted_iota(jnp.int32, (rows.shape[0], AUX), 1)
    block = jnp.where(spot == 0, high, jnp.where(spot == 1, squares - high, 0.0))
    scratch[:, width:] = block
    rows = (rows * gain[...]).astype(bf16)
    scratch[:, :width] = jnp.dot(rows, weight[...], preferred_element_type=f32)
    split(scratch, index[0], own, [one, two, three])


def local(kernel, outs, scratch, index, *args):
    return pl.pallas_call(
        kernel,
        out_shape=[kind(shape, dtype) for kind, shape, dtype in outs],
        in_specs=[pl.BlockSpec(memory_space=pltpu.SMEM)] + [VMEM] * len(args),
        out_specs=[VMEM] * len(outs),
        scratch_shapes=[pltpu.VMEM(scratch, f32)],
        compiler_params=pltpu.CompilerParams(vmem_limit_bytes=24 * 1024 * 1024),
    )(index, *args)


def shards(scan_out, gate_in, norm_gain, w_out, resid, mlp_gain, w_up, w_down, cotangent):
    it, ix, ic = lax.axis_index("tok"), lax.axis_index("x"), lax.axis_index("core")
    iy, iz = lax.axis_index("y"), lax.axis_index("zh")
    group_width = INNER // GROUPS
    units, feats = w_out.shape
    cat = jnp.concatenate

    def one_hot(at_home, at_norm):
        home = (
            ((it ^ ((at_home >> 3) & 3)) << 6)
            | ((ix ^ ((at_home >> 5) & 3)) << 4)
            | ((ic ^ (at_home >> 7)) << 3)
            | (at_home & 7)
        )
        norm = ((iy ^ (at_norm >> 6)) << 6) | ((iz ^ ((at_norm >> 5) & 1)) << 5) | (at_norm & 31)
        return (home == norm).astype(bf16)

    across = lax.broadcasted_iota(jnp.int32, (256, 256), 1)
    along = lax.broadcasted_iota(jnp.int32, (256, 256), 0)
    to_home, to_norm = one_hot(along, across), one_hot(across, along)

    scan_float = scan_out.astype(f32)
    gate_float = gate_in.astype(f32)
    logistic = jax.nn.sigmoid(gate_float)
    gated_unit = gate_float * logistic
    product = scan_float * gated_unit
    squares = jnp.sum(product * product, axis=1, keepdims=True)
    rows = cat([(product * norm_gain[None, :]).astype(bf16), columns(squares)], axis=1)
    rows = cat([rows, swapped(rows, "zh", 1)])
    rows = cat(around(rows, "y"))
    rows = jnp.dot(to_home, rows, preferred_element_type=f32)
    squares = column(rows[:, units:], 0)
    product_all = rows[:, :units].astype(bf16)

    partial = jnp.dot(product_all[128:], w_out, preferred_element_type=f32)
    spot = lax.broadcasted_iota(jnp.int32, (128, AUX), 1)
    other = swapped(cat([partial, jnp.where(spot == 0, squares[128:], 0.0)], axis=1), "core", 1)
    partial = jnp.dot(product_all[:128], w_out, preferred_element_type=f32) + other[:, :feats]
    squares = squares[:128] + other[:, feats : feats + 1]
    packed = cat([partial.astype(bf16), columns(squares)], axis=1)
    parts = [packed] + sent([packed[32 * d : 32 * d + 32] for d in range(4)], "x")
    parts = [part[:32].astype(f32) for part in parts]
    near, far = parts[0] + parts[1], parts[2] + parts[3]
    scale_near = lax.rsqrt(column(near[:, feats:], 0) / group_width + epsilon)
    scale_far = lax.rsqrt(column(far[:, feats:], 0) / group_width + epsilon)
    near, far = near[:, :feats] * scale_near, far[:, :feats] * scale_far
    summed = near + far
    summed = cat([summed[:8] + resid.astype(f32), summed[8:]]).astype(bf16)
    parts = around(cat([summed, cotangent]), "tok")
    cot_tok = cat([part[32:] for part in parts])
    stream = lax.reduce_precision(total([turned(parts[d][:32], d) for d in range(4)]), 8, 7)
    parts = around(cat([stream.astype(bf16), cot_tok, columns(scale_near, scale_far)], axis=1), "x")
    scales = [column(parts[d][:, 2 * feats :], d // 2) for d in range(4)]
    rows = cat([part[:, : 2 * feats] for part in parts])
    rows = cat([rows, columns(cat(scales))], axis=1)
    far_rows = swapped(rows, "core", 1)
    group_scale = column(cat([rows[:, 2 * feats :], far_rows[:, 2 * feats :]]), 0)
    mixed = (product_all.astype(f32) * group_scale).astype(bf16)

    width = w_up.shape[1]
    index = iy.astype(jnp.int32).reshape(1)
    outs = [(pltpu.VMEM, (64, width), f32)] + [(pltpu.VMEM, (64, width), bf16)] * 3
    back = local(slope_kernel, outs, (256, width), index, rows, far_rows, w_down)
    back = total([back[0]] + sent(back, "y"))
    back = back + swapped(back.astype(bf16), "zh", 1).astype(f32)
    back = placed(around(back.astype(bf16), "y"), iy)

    outs = [(pltpu.VMEM, (64, width + AUX), f32)] + [(pltpu.VMEM, (64, width + AUX), bf16)] * 3
    outs += [(jax.ShapeDtypeStruct, (256, feats), bf16)] * 2
    *raw, rows, cot = local(
        raw_kernel, outs, (256, width + AUX), index, rows, far_rows, mlp_gain[None, :], w_up
    )
    rows_float = rows.astype(f32)
    parts = sent(raw, "y")
    raw = total(raw[:1] + parts)
    raw, squares = raw[:, :width], column(raw[:, width:], 0)
    other = swapped(cat([raw.astype(bf16), columns(squares)], axis=1), "zh", 1)
    squares = squares + column(other[:, width:], 0)
    stream_scale = lax.rsqrt(squares / D + epsilon)
    pre = (raw + other[:, :width].astype(f32)) * stream_scale
    pre = placed(around(cat([pre.astype(bf16), columns(stream_scale)], axis=1), "y"), iy)
    scales = column(pre[:, width:], 0)
    active = jax.nn.relu(pre[:, :width].astype(f32))
    squared = jnp.square(active).astype(bf16)
    slope = 2.0 * active * back.astype(f32)
    delta = slope.astype(bf16)
    inner = jnp.sum(slope * active, axis=1, keepdims=True)

    def down_half(rows):
        return jnp.dot(rows, w_down, preferred_element_type=f32).astype(bf16)

    up_back = contract_cols(delta[128:], w_up).astype(bf16)
    inner = columns(inner)
    other = swapped(cat([up_back, down_half(squared[128:]), inner[128:]], axis=1), "core", 1)
    other = other.astype(f32)
    up_back = contract_cols(delta[:128], w_up) + other[:, :feats]
    down = other[:, feats : 2 * feats]
    inner = columns(column(inner[:128].astype(f32) + other[:, 2 * feats :], 0))
    packed = cat([up_back.astype(bf16), inner], axis=1)
    packed, squared = lax.optimization_barrier((packed, squared))
    parts = [packed[:32]] + sent([packed[32 * d : 32 * d + 32] for d in range(4)], "x")
    down = (down_half(squared[:128]).astype(f32) + down).astype(bf16)
    grad_w_down = contract_rows(squared, cot).astype(bf16)
    mine = total(parts)
    mine = cat([mine[:, :feats].astype(bf16), columns(column(mine[:, feats:], 0))], axis=1)
    mine, grad_w_down = lax.optimization_barrier((mine, grad_w_down))
    parts = around(mine, "tok")
    mine = total([turned(parts[d], d) for d in range(4)])
    up_back, inner = mine[:, :feats], column(mine[:, feats:], 0)
    own_scale = scales[:32]
    unit = stream * own_scale
    unit_back = up_back * mlp_gain[None, :]
    grads = lax.reduce_precision(
        cot_tok.astype(f32) + own_scale * (unit_back - unit * (inner / D)), 8, 7
    )
    grad_resid = grads[:8].astype(bf16)
    dot_near = jnp.sum(grads * near, axis=1, keepdims=True)
    dot_far = jnp.sum(grads * far, axis=1, keepdims=True)
    gain_sum = lines(jnp.sum(up_back * unit, axis=0, keepdims=True), feats + AUX)
    packed = cat([grads.astype(bf16), columns(dot_near, dot_far)], axis=1)
    packed = cat([packed, gain_sum])
    packed, delta = lax.optimization_barrier((packed, delta))
    parts = around(packed, "x")
    up_in = (rows_float * scales * mlp_gain[None, :]).astype(bf16)
    grad_w_up = contract_rows(up_in, delta).astype(bf16)
    gain_sum = lines(total([line(part[32:, :feats]) for part in parts]), feats + AUX)
    packed = cat([part[:32] for part in parts] + [gain_sum])
    packed, grad_w_up = lax.optimization_barrier((packed, grad_w_up))
    other = swapped(packed, "core", 1)
    grad_mlp_gain = (line(gain_sum) + line(other[128:]))[0, :feats]
    packed = cat([packed[:128], other[:128]])
    grads, dots = packed[:, :feats], either(packed[:, feats:])

    mixed_back = contract_cols(grads, w_out)
    gain_sum = jnp.sum(mixed_back * mixed.astype(f32), axis=0, keepdims=True)
    gain_sum = lines(gain_sum, units + AUX)
    rows = cat([mixed_back.astype(bf16), columns(dots, group_scale)], axis=1)
    rows = jnp.dot(to_norm, rows, preferred_element_type=f32).astype(bf16)
    group_scale = column(rows[:32, units:], 1)
    parts = [cat([rows[64 * d : 64 * d + 64], gain_sum]) for d in range(4)]
    parts, down, mixed, grads = lax.optimization_barrier((parts, down, mixed, grads))
    parts = parts[:1] + sent(parts, "y")
    down = [down[:32]] + sent([down[32 * d : 32 * d + 32] for d in range(4)], "x")
    summed = total(parts)
    mixed_back, gain_sum = summed[:64], lines(summed[64:65] + summed[65:66], units + AUX)
    dots = column(mixed_back[:, units:], 0)
    down = jnp.where(dots[:32] == dots[:32], total(down), 0.0)
    packed = cat([mixed_back[32:, :units].astype(bf16), columns(dots[32:])], axis=1)
    packed = cat([packed, gain_sum])
    other = swapped(packed, "zh", 1)
    parts = [down[:8]] + sent([down[8 * d : 8 * d + 8].astype(bf16) for d in range(4)], "tok")
    parts, gain_other = lax.optimization_barrier((parts, other[32:]))
    block_out = (stream[:8] + total(parts)).astype(bf16)
    grad_w_out = contract_rows(mixed, grads).astype(bf16)
    mixed_back = mixed_back[:32, :units] + other[:32, :units].astype(f32)
    dots = dots[:32] + column(other[:32, units:], 0)
    grad_norm_gain = (line(gain_sum) + line(gain_other))[0, :units] / norm_gain
    normed = product * group_scale
    product_back = group_scale * (mixed_back * norm_gain[None, :] - normed * (dots / group_width))
    grad_scan = (product_back * gated_unit).astype(bf16)
    grad_gate = (
        product_back * scan_float * logistic * (1.0 + gate_float * (1.0 - logistic))
    ).astype(bf16)
    return (
        block_out,
        grad_scan,
        grad_gate,
        grad_norm_gain,
        grad_w_out,
        grad_resid,
        grad_mlp_gain,
        grad_w_up,
        grad_w_down,
    )


def solution(mesh):
    fine = Mesh(mesh.devices.reshape(4, 4, 2, 4, 2), ("tok", "x", "core", "y", "zh"))
    tk, nout = ("tok", "x", "core"), ("y", "zh")
    in_specs = (
        P(nout, tk),
        P(nout, tk),
        P(tk),
        P(tk, nout),
        P(tk, nout),
        P(nout),
        P(nout, tk),
        P(tk, nout),
        P(tk, nout),
    )
    out_specs = (
        P(tk, nout),
        P(nout, tk),
        P(nout, tk),
        P(tk),
        P(tk, nout),
        P(tk, nout),
        P(nout),
        P(nout, tk),
        P(tk, nout),
    )
    return jax.shard_map(shards, mesh=fine, in_specs=in_specs, out_specs=out_specs, check_vma=False)
```

```python
import jax
import jax.numpy as jnp
from jax import lax
from jax.experimental import pallas as pl
from jax.experimental.layout import Layout, with_layout_constraint
from jax.experimental.pallas import tpu as pltpu
from jax.sharding import Mesh, PartitionSpec as P

D = 8192
INNER = 16384
GROUPS = 8
AUX = 128

epsilon = 1e-05
f32 = jnp.float32
bf16 = jnp.bfloat16


def rowed(value):
    return with_layout_constraint(value, Layout(major_to_minor=tuple(range(value.ndim))))


def swapped(value, axis, mask):
    pairs = [(i, i ^ mask) for i in range(lax.axis_size(axis))]
    return rowed(lax.ppermute(rowed(value), axis, pairs))


def sent(pieces, axis):
    second, third, first = [swapped(pieces[d], axis, d) for d in (2, 3, 1)]
    return [first, second, third]


def around(value, axis):
    return [value] + sent([value] * 4, axis)


def placed(parts, index):
    bit = 1
    while bit < len(parts):
        flip = (index & bit) != 0
        parts = [jnp.where(flip, parts[j ^ bit], parts[j]) for j in range(len(parts))]
        bit *= 2
    return jnp.concatenate(parts)


def total(parts):
    first, second, third, fourth = [part.astype(f32) for part in parts]
    return (first + second) + (third + fourth)


def halves(value):
    high = lax.reduce_precision(value, 8, 7)
    return high, value - high


def columns(*values):
    rows = values[0].shape[0]
    spot = lax.broadcasted_iota(jnp.int32, (rows, AUX), 1)
    block = jnp.zeros((rows, AUX), f32)
    for k, value in enumerate(values):
        high, low = halves(value)
        block = jnp.where(spot == 2 * k, high, block)
        block = jnp.where(spot == 2 * k + 1, low, block)
    return block.astype(bf16)


def column(block, k):
    return block[:, 2 * k : 2 * k + 1].astype(f32) + block[:, 2 * k + 1 : 2 * k + 2].astype(f32)


def lines(value, width):
    high, low = halves(value)
    spot = lax.broadcasted_iota(jnp.int32, (16, value.shape[1]), 0)
    block = jnp.where(spot == 0, high, jnp.where(spot == 1, low, 0.0)).astype(bf16)
    return jnp.pad(block, ((0, 0), (0, width - value.shape[1])))


def line(block):
    return block[0:1].astype(f32) + block[1:2].astype(f32)


def either(block):
    rows = lax.broadcasted_iota(jnp.int32, (block.shape[0], 1), 0)
    return jnp.where((rows & 64) == 0, column(block, 0), column(block, 1))


def turned(value, mask):
    return jnp.concatenate([value[8 * (j ^ mask) : 8 * (j ^ mask) + 8] for j in range(4)])


def contract_rows(left, right):
    return lax.dot_general(left, right, (((0,), (0,)), ((), ())), preferred_element_type=f32)


def contract_cols(left, right):
    return lax.dot_general(left, right, (((1,), (1,)), ((), ())), preferred_element_type=f32)


VMEM = pl.BlockSpec(memory_space=pltpu.VMEM)


def split(scratch, index, own, pieces):
    rows = own.shape[0]
    for d, piece in enumerate([own] + pieces):
        block = scratch[pl.ds(pl.multiple_of((index ^ d) * rows, rows), rows), :]
        piece[...] = block.astype(piece.dtype)


def both_halves(near, far, start, stop):
    return jnp.concatenate([near[:, start:stop], far[:, start:stop]])


def columned(value):
    high = value.astype(bf16).astype(f32)
    spot = lax.broadcasted_iota(jnp.int32, (value.shape[0], AUX), 1)
    return jnp.where(spot == 0, high, jnp.where(spot == 1, value - high, 0.0))


def front_kernel(index, near, far, gain, w_down, w_up, *refs):
    back, raw, (rows_out, cot_out, back_all, raw_all) = refs[:4], refs[4:8], refs[8:]
    feats, width = w_up.shape
    cot = both_halves(near, far, feats, 2 * feats)
    cot_out[...] = cot
    back_all[...] = contract_cols(cot, w_down[...])
    split(back_all, index[0], back[0], list(back[1:]))
    rows = both_halves(near, far, 0, feats)
    rows_out[...] = rows
    rows = rows.astype(f32)
    raw_all[:, width:] = columned(jnp.sum(rows * rows, axis=1, keepdims=True))
    rows = (rows * gain[...]).astype(bf16)
    raw_all[:, :width] = jnp.dot(rows, w_up[...], preferred_element_type=f32)
    split(raw_all, index[0], raw[0], list(raw[1:]))


def hidden_kernel(index, *refs):
    pre, back, (w_down, w_up) = refs[:4], refs[4:8], refs[8:10]
    packed, near, squared, delta, scales, inner = refs[10:]
    feats, width = w_up.shape
    for d in range(4):
        rows = pl.ds(pl.multiple_of((index[0] ^ d) * 64, 64), 64)
        active = jnp.maximum(pre[d][:, :width].astype(f32), 0.0)
        slope = 2.0 * active * back[d][...].astype(f32)
        squared[rows, :] = (active * active).astype(bf16)
        delta[rows, :] = slope.astype(bf16)
        scales[rows, :] = pre[d][:, width:]
        inner[rows, :] = columned(jnp.sum(slope * active, axis=1, keepdims=True))
    near[...] = inner[:128, :]
    packed[:, :feats] = contract_cols(delta[128:, :], w_up[...]).astype(bf16)
    down = jnp.dot(squared[128:, :], w_down[...], preferred_element_type=f32)
    packed[:, feats : 2 * feats] = down.astype(bf16)
    packed[:, 2 * feats :] = inner[128:, :].astype(bf16)


def local(kernel, outs, scratch, index, *args):
    return pl.pallas_call(
        kernel,
        out_shape=[kind(shape, dtype) for kind, shape, dtype in outs],
        in_specs=[pl.BlockSpec(memory_space=pltpu.SMEM)] + [VMEM] * len(args),
        out_specs=[VMEM] * len(outs),
        scratch_shapes=[pltpu.VMEM(shape, f32) for shape in scratch],
        compiler_params=pltpu.CompilerParams(vmem_limit_bytes=24 * 1024 * 1024),
    )(index, *args)


def shards(scan_out, gate_in, norm_gain, w_out, resid, mlp_gain, w_up, w_down, cotangent):
    it, ix, ic = lax.axis_index("tok"), lax.axis_index("x"), lax.axis_index("core")
    iy, iz = lax.axis_index("y"), lax.axis_index("zh")
    group_width = INNER // GROUPS
    units, feats = w_out.shape
    cat = jnp.concatenate

    def one_hot(at_home, at_norm):
        home = (
            ((it ^ ((at_home >> 3) & 3)) << 6)
            | ((ix ^ ((at_home >> 5) & 3)) << 4)
            | ((ic ^ (at_home >> 7)) << 3)
            | (at_home & 7)
        )
        norm = ((iy ^ (at_norm >> 6)) << 6) | ((iz ^ ((at_norm >> 5) & 1)) << 5) | (at_norm & 31)
        return (home == norm).astype(bf16)

    across = lax.broadcasted_iota(jnp.int32, (256, 256), 1)
    along = lax.broadcasted_iota(jnp.int32, (256, 256), 0)
    to_home, to_norm = one_hot(along, across), one_hot(across, along)

    scan_float = scan_out.astype(f32)
    gate_float = gate_in.astype(f32)
    logistic = jax.nn.sigmoid(gate_float)
    gated_unit = gate_float * logistic
    product = scan_float * gated_unit
    squares = jnp.sum(product * product, axis=1, keepdims=True)
    rows = cat([(product * norm_gain[None, :]).astype(bf16), columns(squares)], axis=1)
    rows = cat([rows, swapped(rows, "zh", 1)])
    rows = cat(around(rows, "y"))
    rows = jnp.dot(to_home, rows, preferred_element_type=f32)
    squares = column(rows[:, units:], 0)
    product_all = rows[:, :units].astype(bf16)

    partial = jnp.dot(product_all[128:], w_out, preferred_element_type=f32)
    spot = lax.broadcasted_iota(jnp.int32, (128, AUX), 1)
    other = swapped(cat([partial, jnp.where(spot == 0, squares[128:], 0.0)], axis=1), "core", 1)
    partial = jnp.dot(product_all[:128], w_out, preferred_element_type=f32) + other[:, :feats]
    squares = squares[:128] + other[:, feats : feats + 1]
    packed = cat([partial.astype(bf16), columns(squares)], axis=1)
    parts = [packed] + sent([packed[32 * d : 32 * d + 32] for d in range(4)], "x")
    parts = [part[:32].astype(f32) for part in parts]
    near, far = parts[0] + parts[1], parts[2] + parts[3]
    scale_near = lax.rsqrt(column(near[:, feats:], 0) / group_width + epsilon)
    scale_far = lax.rsqrt(column(far[:, feats:], 0) / group_width + epsilon)
    near, far = near[:, :feats] * scale_near, far[:, :feats] * scale_far
    summed = near + far
    summed = cat([summed[:8] + resid.astype(f32), summed[8:]]).astype(bf16)
    parts = around(cat([summed, cotangent]), "tok")
    cot_tok = cat([part[32:] for part in parts])
    stream = lax.reduce_precision(total([turned(parts[d][:32], d) for d in range(4)]), 8, 7)
    parts = around(cat([stream.astype(bf16), cot_tok, columns(scale_near, scale_far)], axis=1), "x")
    rows = cat(parts)
    far_rows = swapped(rows, "core", 1)
    group_scale = either(cat([rows[:, 2 * feats :], far_rows[:, 2 * feats :]]))
    mixed = (product_all.astype(f32) * group_scale).astype(bf16)

    width = w_up.shape[1]
    index = iy.astype(jnp.int32).reshape(1)
    outs = [(pltpu.VMEM, (64, width), f32)] + [(pltpu.VMEM, (64, width), bf16)] * 3
    outs += [(pltpu.VMEM, (64, width + AUX), f32)] + [(pltpu.VMEM, (64, width + AUX), bf16)] * 3
    outs += [(jax.ShapeDtypeStruct, (256, feats), bf16)] * 2
    scratch = [(256, width), (256, width + AUX)]
    fronts = local(
        front_kernel, outs, scratch, index, rows, far_rows, mlp_gain[None, :], w_down, w_up
    )
    back, raw, (rows, cot) = fronts[:4], fronts[4:8], fronts[8:]
    rows_float = rows.astype(f32)
    back = total([back[0]] + sent(back, "y"))
    back = back + swapped(back.astype(bf16), "zh", 1).astype(f32)
    back = around(back.astype(bf16), "y")
    parts = sent(raw, "y")
    raw = total([raw[0]] + parts)
    raw, squares = raw[:, :width], column(raw[:, width:], 0)
    other = swapped(cat([raw.astype(bf16), columns(squares)], axis=1), "zh", 1)
    other, back = lax.optimization_barrier((other, back))
    squares = squares + column(other[:, width:], 0)
    stream_scale = lax.rsqrt(squares / D + epsilon)
    pre = (raw + other[:, :width].astype(f32)) * stream_scale
    pre = around(cat([pre.astype(bf16), columns(stream_scale)], axis=1), "y")
    outs = [(pltpu.VMEM, (128, 2 * feats + AUX), bf16), (pltpu.VMEM, (128, AUX), f32)]
    outs += [(jax.ShapeDtypeStruct, (256, width), bf16)] * 2
    outs += [(jax.ShapeDtypeStruct, (256, AUX), bf16)]
    packed, inner, squared, delta, scales = local(
        hidden_kernel, outs, [(256, AUX)], index, *pre, *back, w_down, w_up
    )
    scales = column(scales, 0)

    def down_half(rows):
        return jnp.dot(rows, w_down, preferred_element_type=f32).astype(bf16)

    other = swapped(packed, "core", 1)
    other = other.astype(f32)
    up_back = contract_cols(delta[:128], w_up) + other[:, :feats]
    down = other[:, feats : 2 * feats]
    inner = columns(column(inner + other[:, 2 * feats :], 0))
    packed = cat([up_back.astype(bf16), inner], axis=1)
    packed, squared = lax.optimization_barrier((packed, squared))
    parts = [packed[:32]] + sent([packed[32 * d : 32 * d + 32] for d in range(4)], "x")
    down = (down_half(squared[:128]).astype(f32) + down).astype(bf16)
    grad_w_down = contract_rows(squared, cot).astype(bf16)
    mine = total(parts)
    mine = cat([mine[:, :feats].astype(bf16), columns(column(mine[:, feats:], 0))], axis=1)
    mine, grad_w_down = lax.optimization_barrier((mine, grad_w_down))
    parts = around(mine, "tok")
    mine = total([turned(parts[d], d) for d in range(4)])
    up_back, inner = mine[:, :feats], column(mine[:, feats:], 0)
    own_scale = scales[:32]
    unit = stream * own_scale
    unit_back = up_back * mlp_gain[None, :]
    grads = lax.reduce_precision(
        cot_tok.astype(f32) + own_scale * (unit_back - unit * (inner / D)), 8, 7
    )
    grad_resid = grads[:8].astype(bf16)
    dot_near = jnp.sum(grads * near, axis=1, keepdims=True)
    dot_far = jnp.sum(grads * far, axis=1, keepdims=True)
    gain_sum = lines(jnp.sum(up_back * unit, axis=0, keepdims=True), feats + AUX)
    packed = cat([grads.astype(bf16), columns(dot_near, dot_far)], axis=1)
    packed = cat([packed, gain_sum])
    packed, delta = lax.optimization_barrier((packed, delta))
    parts = around(packed, "x")
    up_in = (rows_float * scales * mlp_gain[None, :]).astype(bf16)
    grad_w_up = contract_rows(up_in, delta).astype(bf16)
    gain_sum = lines(total([line(part[32:, :feats]) for part in parts]), feats + AUX)
    packed = cat([part[:32] for part in parts] + [gain_sum])
    packed, grad_w_up = lax.optimization_barrier((packed, grad_w_up))
    other = swapped(packed, "core", 1)
    grad_mlp_gain = (line(gain_sum) + line(other[128:]))[0, :feats]
    packed = cat([packed[:128], other[:128]])
    grads, dots = packed[:, :feats], either(packed[:, feats:])

    mixed_back = contract_cols(grads, w_out)
    gain_sum = jnp.sum(mixed_back * mixed.astype(f32), axis=0, keepdims=True)
    gain_sum = lines(gain_sum, units + AUX)
    rows = cat([mixed_back.astype(bf16), columns(dots, group_scale)], axis=1)
    rows = jnp.dot(to_norm, rows, preferred_element_type=f32).astype(bf16)
    group_scale = column(rows[:32, units:], 1)
    parts = [cat([rows[64 * d : 64 * d + 64], gain_sum]) for d in range(4)]
    parts, down, mixed, grads = lax.optimization_barrier((parts, down, mixed, grads))
    parts = parts[:1] + sent(parts, "y")
    down = [down[:32]] + sent([down[32 * d : 32 * d + 32] for d in range(4)], "x")
    summed = total(parts)
    mixed_back, gain_sum = summed[:64], lines(summed[64:65] + summed[65:66], units + AUX)
    dots = column(mixed_back[:, units:], 0)
    down = jnp.where(dots[:32] == dots[:32], total(down), 0.0)
    packed = cat([mixed_back[32:, :units].astype(bf16), columns(dots[32:])], axis=1)
    packed = cat([packed, gain_sum])
    other = swapped(packed, "zh", 1)
    parts = [down[:8]] + sent([down[8 * d : 8 * d + 8].astype(bf16) for d in range(4)], "tok")
    parts, gain_other = lax.optimization_barrier((parts, other[32:]))
    block_out = (stream[:8] + total(parts)).astype(bf16)
    grad_w_out = contract_rows(mixed, grads).astype(bf16)
    mixed_back = mixed_back[:32, :units] + other[:32, :units].astype(f32)
    dots = dots[:32] + column(other[:32, units:], 0)
    grad_norm_gain = (line(gain_sum) + line(gain_other))[0, :units] / norm_gain
    normed = product * group_scale
    product_back = group_scale * (mixed_back * norm_gain[None, :] - normed * (dots / group_width))
    grad_scan = (product_back * gated_unit).astype(bf16)
    grad_gate = (
        product_back * scan_float * logistic * (1.0 + gate_float * (1.0 - logistic))
    ).astype(bf16)
    return (
        block_out,
        grad_scan,
        grad_gate,
        grad_norm_gain,
        grad_w_out,
        grad_resid,
        grad_mlp_gain,
        grad_w_up,
        grad_w_down,
    )


def solution(mesh):
    fine = Mesh(mesh.devices.reshape(4, 4, 2, 4, 2), ("tok", "x", "core", "y", "zh"))
    tk, nout = ("tok", "x", "core"), ("y", "zh")
    in_specs = (
        P(nout, tk),
        P(nout, tk),
        P(tk),
        P(tk, nout),
        P(tk, nout),
        P(nout),
        P(nout, tk),
        P(tk, nout),
        P(tk, nout),
    )
    out_specs = (
        P(tk, nout),
        P(nout, tk),
        P(nout, tk),
        P(tk),
        P(tk, nout),
        P(tk, nout),
        P(nout),
        P(nout, tk),
        P(tk, nout),
    )
    return jax.shard_map(shards, mesh=fine, in_specs=in_specs, out_specs=out_specs, check_vma=False)
```

```python
import jax
import jax.numpy as jnp
from jax import lax
from jax.experimental import pallas as pl
from jax.experimental.layout import Layout, with_layout_constraint
from jax.experimental.pallas import tpu as pltpu
from jax.sharding import Mesh, PartitionSpec as P

D = 8192
INNER = 16384
GROUPS = 8
AUX = 128

epsilon = 1e-05
f32 = jnp.float32
bf16 = jnp.bfloat16


def rowed(value):
    return with_layout_constraint(value, Layout(major_to_minor=tuple(range(value.ndim))))


def swapped(value, axis, mask):
    pairs = [(i, i ^ mask) for i in range(lax.axis_size(axis))]
    return rowed(lax.ppermute(rowed(value), axis, pairs))


def sent(pieces, axis):
    second, third, first = [swapped(pieces[d], axis, d) for d in (2, 3, 1)]
    return [first, second, third]


def around(value, axis):
    return [value] + sent([value] * 4, axis)


def placed(parts, index):
    bit = 1
    while bit < len(parts):
        flip = (index & bit) != 0
        parts = [jnp.where(flip, parts[j ^ bit], parts[j]) for j in range(len(parts))]
        bit *= 2
    return jnp.concatenate(parts)


def total(parts):
    first, second, third, fourth = [part.astype(f32) for part in parts]
    return (first + second) + (third + fourth)


def halves(value):
    high = lax.reduce_precision(value, 8, 7)
    return high, value - high


def columns(*values):
    rows = values[0].shape[0]
    spot = lax.broadcasted_iota(jnp.int32, (rows, AUX), 1)
    block = jnp.zeros((rows, AUX), f32)
    for k, value in enumerate(values):
        high, low = halves(value)
        block = jnp.where(spot == 2 * k, high, block)
        block = jnp.where(spot == 2 * k + 1, low, block)
    return block.astype(bf16)


def column(block, k):
    return block[:, 2 * k : 2 * k + 1].astype(f32) + block[:, 2 * k + 1 : 2 * k + 2].astype(f32)


def lines(value, width):
    high, low = halves(value)
    spot = lax.broadcasted_iota(jnp.int32, (16, value.shape[1]), 0)
    block = jnp.where(spot == 0, high, jnp.where(spot == 1, low, 0.0)).astype(bf16)
    return jnp.pad(block, ((0, 0), (0, width - value.shape[1])))


def line(block):
    return block[0:1].astype(f32) + block[1:2].astype(f32)


def either(block):
    rows = lax.broadcasted_iota(jnp.int32, (block.shape[0], 1), 0)
    return jnp.where((rows & 64) == 0, column(block, 0), column(block, 1))


def turned(value, mask):
    return jnp.concatenate([value[8 * (j ^ mask) : 8 * (j ^ mask) + 8] for j in range(4)])


def contract_rows(left, right):
    return lax.dot_general(left, right, (((0,), (0,)), ((), ())), preferred_element_type=f32)


def contract_cols(left, right):
    return lax.dot_general(left, right, (((1,), (1,)), ((), ())), preferred_element_type=f32)


VMEM = pl.BlockSpec(memory_space=pltpu.VMEM)


def split(scratch, index, own, pieces):
    rows = own.shape[0]
    for d, piece in enumerate([own] + pieces):
        block = scratch[pl.ds(pl.multiple_of((index ^ d) * rows, rows), rows), :]
        piece[...] = block.astype(piece.dtype)


def both_halves(near, far, start, stop):
    return jnp.concatenate([near[:, start:stop], far[:, start:stop]])


def columned(value):
    high = value.astype(bf16).astype(f32)
    spot = lax.broadcasted_iota(jnp.int32, (value.shape[0], AUX), 1)
    return jnp.where(spot == 0, high, jnp.where(spot == 1, value - high, 0.0))


def front_kernel(index, near, far, gain, w_down, w_up, *refs):
    back, raw, (rows_out, cot_out, back_all, raw_all) = refs[:4], refs[4:8], refs[8:]
    feats, width = w_up.shape
    cot = both_halves(near, far, feats, 2 * feats)
    cot_out[...] = cot
    back_all[...] = contract_cols(cot, w_down[...])
    split(back_all, index[0], back[0], list(back[1:]))
    rows = both_halves(near, far, 0, feats)
    rows_out[...] = rows
    rows = rows.astype(f32)
    raw_all[:, width:] = columned(jnp.sum(rows * rows, axis=1, keepdims=True))
    rows = (rows * gain[...]).astype(bf16)
    raw_all[:, :width] = jnp.dot(rows, w_up[...], preferred_element_type=f32)
    split(raw_all, index[0], raw[0], list(raw[1:]))


def hidden_kernel(index, *refs):
    pre, (back, w_down, w_up) = refs[:4], refs[4:7]
    packed, near, squared, delta, scales, inner = refs[7:]
    feats, width = w_up.shape
    for d in range(4):
        rows = pl.ds(pl.multiple_of((index[0] ^ d) * 64, 64), 64)
        active = jnp.maximum(pre[d][:, :width].astype(f32), 0.0)
        slope = 2.0 * active * back[64 * d : 64 * d + 64, :].astype(f32)
        squared[rows, :] = (active * active).astype(bf16)
        delta[rows, :] = slope.astype(bf16)
        scales[rows, :] = pre[d][:, width:]
        inner[rows, :] = columned(jnp.sum(slope * active, axis=1, keepdims=True))
    near[...] = inner[:128, :]
    packed[:, :feats] = contract_cols(delta[128:, :], w_up[...]).astype(bf16)
    down = jnp.dot(squared[128:, :], w_down[...], preferred_element_type=f32)
    packed[:, feats : 2 * feats] = down.astype(bf16)
    packed[:, 2 * feats :] = inner[128:, :].astype(bf16)


def local(kernel, outs, scratch, index, *args):
    return pl.pallas_call(
        kernel,
        out_shape=[kind(shape, dtype) for kind, shape, dtype in outs],
        in_specs=[pl.BlockSpec(memory_space=pltpu.SMEM)] + [VMEM] * len(args),
        out_specs=[VMEM] * len(outs),
        scratch_shapes=[pltpu.VMEM(shape, f32) for shape in scratch],
        compiler_params=pltpu.CompilerParams(vmem_limit_bytes=24 * 1024 * 1024),
    )(index, *args)


def shards(scan_out, gate_in, norm_gain, w_out, resid, mlp_gain, w_up, w_down, cotangent):
    it, ix, ic = lax.axis_index("tok"), lax.axis_index("x"), lax.axis_index("core")
    iy, iz = lax.axis_index("y"), lax.axis_index("zh")
    group_width = INNER // GROUPS
    units, feats = w_out.shape
    cat = jnp.concatenate

    def one_hot(at_home, at_norm):
        home = (
            ((it ^ ((at_home >> 3) & 3)) << 6)
            | ((ix ^ ((at_home >> 5) & 3)) << 4)
            | ((ic ^ (at_home >> 7)) << 3)
            | (at_home & 7)
        )
        norm = ((iy ^ (at_norm >> 6)) << 6) | ((iz ^ ((at_norm >> 5) & 1)) << 5) | (at_norm & 31)
        return (home == norm).astype(bf16)

    across = lax.broadcasted_iota(jnp.int32, (256, 256), 1)
    along = lax.broadcasted_iota(jnp.int32, (256, 256), 0)
    to_home, to_norm = one_hot(along, across), one_hot(across, along)

    scan_float = scan_out.astype(f32)
    gate_float = gate_in.astype(f32)
    logistic = jax.nn.sigmoid(gate_float)
    gated_unit = gate_float * logistic
    product = scan_float * gated_unit
    squares = jnp.sum(product * product, axis=1, keepdims=True)
    rows = cat([(product * norm_gain[None, :]).astype(bf16), columns(squares)], axis=1)
    rows = cat([rows, swapped(rows, "zh", 1)])
    rows = cat(around(rows, "y"))
    rows = jnp.dot(to_home, rows, preferred_element_type=f32)
    squares = column(rows[:, units:], 0)
    product_all = rows[:, :units].astype(bf16)

    partial = jnp.dot(product_all[128:], w_out, preferred_element_type=f32)
    spot = lax.broadcasted_iota(jnp.int32, (128, AUX), 1)
    other = swapped(cat([partial, jnp.where(spot == 0, squares[128:], 0.0)], axis=1), "core", 1)
    partial = jnp.dot(product_all[:128], w_out, preferred_element_type=f32) + other[:, :feats]
    squares = squares[:128] + other[:, feats : feats + 1]
    packed = cat([partial.astype(bf16), columns(squares)], axis=1)
    parts = [packed] + sent([packed[32 * d : 32 * d + 32] for d in range(4)], "x")
    parts = [part[:32].astype(f32) for part in parts]
    near, far = parts[0] + parts[1], parts[2] + parts[3]
    scale_near = lax.rsqrt(column(near[:, feats:], 0) / group_width + epsilon)
    scale_far = lax.rsqrt(column(far[:, feats:], 0) / group_width + epsilon)
    near, far = near[:, :feats] * scale_near, far[:, :feats] * scale_far
    summed = near + far
    summed = cat([summed[:8] + resid.astype(f32), summed[8:]]).astype(bf16)
    parts = around(cat([summed, cotangent]), "tok")
    cot_tok = cat([part[32:] for part in parts])
    stream = lax.reduce_precision(total([turned(parts[d][:32], d) for d in range(4)]), 8, 7)
    parts = around(cat([stream.astype(bf16), cot_tok, columns(scale_near, scale_far)], axis=1), "x")
    rows = cat(parts)
    far_rows = swapped(rows, "core", 1)
    group_scale = either(cat([rows[:, 2 * feats :], far_rows[:, 2 * feats :]]))
    mixed = (product_all.astype(f32) * group_scale).astype(bf16)

    width = w_up.shape[1]
    index = iy.astype(jnp.int32).reshape(1)
    outs = [(pltpu.VMEM, (64, width), f32)] + [(pltpu.VMEM, (64, width), bf16)] * 3
    outs += [(pltpu.VMEM, (64, width + AUX), f32)] + [(pltpu.VMEM, (64, width + AUX), bf16)] * 3
    outs += [(jax.ShapeDtypeStruct, (256, feats), bf16)] * 2
    scratch = [(256, width), (256, width + AUX)]
    fronts = local(
        front_kernel, outs, scratch, index, rows, far_rows, mlp_gain[None, :], w_down, w_up
    )
    back, raw, (rows, cot) = fronts[:4], fronts[4:8], fronts[8:]
    rows_float = rows.astype(f32)
    back = total([back[0]] + sent(back, "y"))
    back = back + swapped(back.astype(bf16), "zh", 1).astype(f32)
    back = cat(around(back.astype(bf16), "y"))
    parts = sent(raw, "y")
    raw = total([raw[0]] + parts)
    raw, squares = raw[:, :width], column(raw[:, width:], 0)
    other = swapped(cat([raw.astype(bf16), columns(squares)], axis=1), "zh", 1)
    squares = squares + column(other[:, width:], 0)
    stream_scale = lax.rsqrt(squares / D + epsilon)
    pre = (raw + other[:, :width].astype(f32)) * stream_scale
    pre = around(cat([pre.astype(bf16), columns(stream_scale)], axis=1), "y")
    pre, back = lax.optimization_barrier((pre, back))
    outs = [(pltpu.VMEM, (128, 2 * feats + AUX), bf16), (pltpu.VMEM, (128, AUX), f32)]
    outs += [(jax.ShapeDtypeStruct, (256, width), bf16)] * 2
    outs += [(jax.ShapeDtypeStruct, (256, AUX), bf16)]
    packed, inner, squared, delta, scales = local(
        hidden_kernel, outs, [(256, AUX)], index, *pre, back, w_down, w_up
    )
    scales = column(scales, 0)

    def down_half(rows):
        return jnp.dot(rows, w_down, preferred_element_type=f32).astype(bf16)

    other = swapped(packed, "core", 1)
    other = other.astype(f32)
    up_back = contract_cols(delta[:128], w_up) + other[:, :feats]
    down = other[:, feats : 2 * feats]
    inner = columns(column(inner + other[:, 2 * feats :], 0))
    packed = cat([up_back.astype(bf16), inner], axis=1)
    packed, squared = lax.optimization_barrier((packed, squared))
    parts = [packed[:32]] + sent([packed[32 * d : 32 * d + 32] for d in range(4)], "x")
    down = (down_half(squared[:128]).astype(f32) + down).astype(bf16)
    grad_w_down = contract_rows(squared, cot).astype(bf16)
    mine = total(parts)
    mine = cat([mine[:, :feats].astype(bf16), columns(column(mine[:, feats:], 0))], axis=1)
    mine, grad_w_down = lax.optimization_barrier((mine, grad_w_down))
    parts = around(mine, "tok")
    mine = total([turned(parts[d], d) for d in range(4)])
    up_back, inner = mine[:, :feats], column(mine[:, feats:], 0)
    own_scale = scales[:32]
    unit = stream * own_scale
    unit_back = up_back * mlp_gain[None, :]
    grads = lax.reduce_precision(
        cot_tok.astype(f32) + own_scale * (unit_back - unit * (inner / D)), 8, 7
    )
    grad_resid = grads[:8].astype(bf16)
    dot_near = jnp.sum(grads * near, axis=1, keepdims=True)
    dot_far = jnp.sum(grads * far, axis=1, keepdims=True)
    gain_sum = lines(jnp.sum(up_back * unit, axis=0, keepdims=True), feats + AUX)
    packed = cat([grads.astype(bf16), columns(dot_near, dot_far)], axis=1)
    packed = cat([packed, gain_sum])
    packed, delta = lax.optimization_barrier((packed, delta))
    parts = around(packed, "x")
    up_in = (rows_float * scales * mlp_gain[None, :]).astype(bf16)
    grad_w_up = contract_rows(up_in, delta).astype(bf16)
    gain_sum = lines(total([line(part[32:, :feats]) for part in parts]), feats + AUX)
    packed = cat([part[:32] for part in parts] + [gain_sum])
    packed, grad_w_up = lax.optimization_barrier((packed, grad_w_up))
    other = swapped(packed, "core", 1)
    grad_mlp_gain = (line(gain_sum) + line(other[128:]))[0, :feats]
    packed = cat([packed[:128], other[:128]])
    grads, dots = packed[:, :feats], either(packed[:, feats:])

    mixed_back = contract_cols(grads, w_out)
    gain_sum = jnp.sum(mixed_back * mixed.astype(f32), axis=0, keepdims=True)
    gain_sum = lines(gain_sum, units + AUX)
    rows = cat([mixed_back.astype(bf16), columns(dots, group_scale)], axis=1)
    rows = jnp.dot(to_norm, rows, preferred_element_type=f32).astype(bf16)
    group_scale = column(rows[:32, units:], 1)
    parts = [cat([rows[64 * d : 64 * d + 64], gain_sum]) for d in range(4)]
    parts, down, mixed, grads = lax.optimization_barrier((parts, down, mixed, grads))
    parts = parts[:1] + sent(parts, "y")
    down = [down[:32]] + sent([down[32 * d : 32 * d + 32] for d in range(4)], "x")
    summed = total(parts)
    mixed_back, gain_sum = summed[:64], lines(summed[64:65] + summed[65:66], units + AUX)
    dots = column(mixed_back[:, units:], 0)
    down = jnp.where(dots[:32] == dots[:32], total(down), 0.0)
    packed = cat([mixed_back[32:, :units].astype(bf16), columns(dots[32:])], axis=1)
    packed = cat([packed, gain_sum])
    other = swapped(packed, "zh", 1)
    parts = [down[:8]] + sent([down[8 * d : 8 * d + 8].astype(bf16) for d in range(4)], "tok")
    parts, gain_other = lax.optimization_barrier((parts, other[32:]))
    block_out = (stream[:8] + total(parts)).astype(bf16)
    grad_w_out = contract_rows(mixed, grads).astype(bf16)
    mixed_back = mixed_back[:32, :units] + other[:32, :units].astype(f32)
    dots = dots[:32] + column(other[:32, units:], 0)
    grad_norm_gain = (line(gain_sum) + line(gain_other))[0, :units] / norm_gain
    normed = product * group_scale
    product_back = group_scale * (mixed_back * norm_gain[None, :] - normed * (dots / group_width))
    grad_scan = (product_back * gated_unit).astype(bf16)
    grad_gate = (
        product_back * scan_float * logistic * (1.0 + gate_float * (1.0 - logistic))
    ).astype(bf16)
    return (
        block_out,
        grad_scan,
        grad_gate,
        grad_norm_gain,
        grad_w_out,
        grad_resid,
        grad_mlp_gain,
        grad_w_up,
        grad_w_down,
    )


def solution(mesh):
    fine = Mesh(mesh.devices.reshape(4, 4, 2, 4, 2), ("tok", "x", "core", "y", "zh"))
    tk, nout = ("tok", "x", "core"), ("y", "zh")
    in_specs = (
        P(nout, tk),
        P(nout, tk),
        P(tk),
        P(tk, nout),
        P(tk, nout),
        P(nout),
        P(nout, tk),
        P(tk, nout),
        P(tk, nout),
    )
    out_specs = (
        P(tk, nout),
        P(nout, tk),
        P(nout, tk),
        P(tk),
        P(tk, nout),
        P(tk, nout),
        P(nout),
        P(nout, tk),
        P(tk, nout),
    )
    return jax.shard_map(shards, mesh=fine, in_specs=in_specs, out_specs=out_specs, check_vma=False)
```

```python
import jax
import jax.numpy as jnp
from jax import lax
from jax.experimental import pallas as pl
from jax.experimental.layout import Layout, with_layout_constraint
from jax.experimental.pallas import tpu as pltpu
from jax.sharding import Mesh, PartitionSpec as P

D = 8192
INNER = 16384
GROUPS = 8
AUX = 128

epsilon = 1e-05
f32 = jnp.float32
bf16 = jnp.bfloat16


def rowed(value):
    return with_layout_constraint(value, Layout(major_to_minor=tuple(range(value.ndim))))


def swapped(value, axis, mask):
    pairs = [(i, i ^ mask) for i in range(lax.axis_size(axis))]
    return rowed(lax.ppermute(rowed(value), axis, pairs))


def sent(pieces, axis):
    second, third, first = [swapped(pieces[d], axis, d) for d in (2, 3, 1)]
    return [first, second, third]


def around(value, axis):
    return [value] + sent([value] * 4, axis)


def placed(parts, index):
    bit = 1
    while bit < len(parts):
        flip = (index & bit) != 0
        parts = [jnp.where(flip, parts[j ^ bit], parts[j]) for j in range(len(parts))]
        bit *= 2
    return jnp.concatenate(parts)


def total(parts):
    first, second, third, fourth = [part.astype(f32) for part in parts]
    return (first + second) + (third + fourth)


def halves(value):
    high = lax.reduce_precision(value, 8, 7)
    return high, value - high


def columns(*values):
    rows = values[0].shape[0]
    spot = lax.broadcasted_iota(jnp.int32, (rows, AUX), 1)
    block = jnp.zeros((rows, AUX), f32)
    for k, value in enumerate(values):
        high, low = halves(value)
        block = jnp.where(spot == 2 * k, high, block)
        block = jnp.where(spot == 2 * k + 1, low, block)
    return block.astype(bf16)


def column(block, k):
    return block[:, 2 * k : 2 * k + 1].astype(f32) + block[:, 2 * k + 1 : 2 * k + 2].astype(f32)


def lines(value, width):
    high, low = halves(value)
    spot = lax.broadcasted_iota(jnp.int32, (16, value.shape[1]), 0)
    block = jnp.where(spot == 0, high, jnp.where(spot == 1, low, 0.0)).astype(bf16)
    return jnp.pad(block, ((0, 0), (0, width - value.shape[1])))


def line(block):
    return block[0:1].astype(f32) + block[1:2].astype(f32)


def either(block):
    rows = lax.broadcasted_iota(jnp.int32, (block.shape[0], 1), 0)
    return jnp.where((rows & 64) == 0, column(block, 0), column(block, 1))


def turned(value, mask):
    return jnp.concatenate([value[8 * (j ^ mask) : 8 * (j ^ mask) + 8] for j in range(4)])


def contract_rows(left, right):
    return lax.dot_general(left, right, (((0,), (0,)), ((), ())), preferred_element_type=f32)


def contract_cols(left, right):
    return lax.dot_general(left, right, (((1,), (1,)), ((), ())), preferred_element_type=f32)


VMEM = pl.BlockSpec(memory_space=pltpu.VMEM)


def split(scratch, index, own, pieces):
    rows = own.shape[0]
    for d, piece in enumerate([own] + pieces):
        block = scratch[pl.ds(pl.multiple_of((index ^ d) * rows, rows), rows), :]
        piece[...] = block.astype(piece.dtype)


def both_halves(near, far, start, stop):
    return jnp.concatenate([near[:, start:stop], far[:, start:stop]])


def columned(value):
    high = value.astype(bf16).astype(f32)
    spot = lax.broadcasted_iota(jnp.int32, (value.shape[0], AUX), 1)
    return jnp.where(spot == 0, high, jnp.where(spot == 1, value - high, 0.0))


def front_kernel(index, near, far, gain, w_down, w_up, *refs):
    back, raw, (rows_out, cot_out, back_all, raw_all) = refs[:4], refs[4:8], refs[8:]
    feats, width = w_up.shape
    cot = both_halves(near, far, feats, 2 * feats)
    cot_out[...] = cot
    back_all[...] = contract_cols(cot, w_down[...])
    split(back_all, index[0], back[0], list(back[1:]))
    rows = both_halves(near, far, 0, feats)
    rows_out[...] = rows
    rows = rows.astype(f32)
    raw_all[:, width:] = columned(jnp.sum(rows * rows, axis=1, keepdims=True))
    rows = (rows * gain[...]).astype(bf16)
    raw_all[:, :width] = jnp.dot(rows, w_up[...], preferred_element_type=f32)
    split(raw_all, index[0], raw[0], list(raw[1:]))


def hidden_kernel(index, *refs):
    pre, (back, w_down, w_up) = refs[:4], refs[4:7]
    packed, near, squared, delta, scales, inner = refs[7:]
    feats, width = w_up.shape
    for d in range(4):
        rows = pl.ds(pl.multiple_of((index[0] ^ d) * 64, 64), 64)
        active = jnp.maximum(pre[d][:, :width].astype(f32), 0.0)
        slope = 2.0 * active * back[64 * d : 64 * d + 64, :].astype(f32)
        squared[rows, :] = (active * active).astype(bf16)
        delta[rows, :] = slope.astype(bf16)
        scales[rows, :] = pre[d][:, width:]
        inner[rows, :] = columned(jnp.sum(slope * active, axis=1, keepdims=True))
    near[...] = inner[:128, :]
    packed[:, :feats] = contract_cols(delta[128:, :], w_up[...]).astype(bf16)
    down = jnp.dot(squared[128:, :], w_down[...], preferred_element_type=f32)
    packed[:, feats : 2 * feats] = down.astype(bf16)
    packed[:, 2 * feats :] = inner[128:, :].astype(bf16)


def local(kernel, outs, scratch, index, *args):
    return pl.pallas_call(
        kernel,
        out_shape=[kind(shape, dtype) for kind, shape, dtype in outs],
        in_specs=[pl.BlockSpec(memory_space=pltpu.SMEM)] + [VMEM] * len(args),
        out_specs=[VMEM] * len(outs),
        scratch_shapes=[pltpu.VMEM(shape, f32) for shape in scratch],
        compiler_params=pltpu.CompilerParams(vmem_limit_bytes=24 * 1024 * 1024),
    )(index, *args)


def shards(scan_out, gate_in, norm_gain, w_out, resid, mlp_gain, w_up, w_down, cotangent):
    it, ix, ic = lax.axis_index("tok"), lax.axis_index("x"), lax.axis_index("core")
    iy, iz = lax.axis_index("y"), lax.axis_index("zh")
    group_width = INNER // GROUPS
    units, feats = w_out.shape
    cat = jnp.concatenate

    def one_hot(at_home, at_norm):
        home = (
            ((it ^ ((at_home >> 3) & 3)) << 6)
            | ((ix ^ ((at_home >> 5) & 3)) << 4)
            | ((ic ^ (at_home >> 7)) << 3)
            | (at_home & 7)
        )
        norm = ((iy ^ (at_norm >> 6)) << 6) | ((iz ^ ((at_norm >> 5) & 1)) << 5) | (at_norm & 31)
        return (home == norm).astype(bf16)

    across = lax.broadcasted_iota(jnp.int32, (256, 256), 1)
    along = lax.broadcasted_iota(jnp.int32, (256, 256), 0)
    to_home, to_norm = one_hot(along, across), one_hot(across, along)

    scan_float = scan_out.astype(f32)
    gate_float = gate_in.astype(f32)
    logistic = jax.nn.sigmoid(gate_float)
    gated_unit = gate_float * logistic
    product = scan_float * gated_unit
    squares = jnp.sum(product * product, axis=1, keepdims=True)
    rows = cat([(product * norm_gain[None, :]).astype(bf16), columns(squares)], axis=1)
    rows = cat([rows, swapped(rows, "zh", 1)])
    rows = cat(around(rows, "y"))
    rows = jnp.dot(to_home, rows, preferred_element_type=f32)
    squares = column(rows[:, units:], 0)
    product_all = rows[:, :units].astype(bf16)

    partial = jnp.dot(product_all[128:], w_out, preferred_element_type=f32)
    other = swapped(cat([partial.astype(bf16), columns(squares[128:])], axis=1), "core", 1)
    other = other.astype(f32)
    partial = jnp.dot(product_all[:128], w_out, preferred_element_type=f32) + other[:, :feats]
    squares = squares[:128] + column(other[:, feats:], 0)
    packed = cat([partial.astype(bf16), columns(squares)], axis=1)
    parts = [packed] + sent([packed[32 * d : 32 * d + 32] for d in range(4)], "x")
    parts = [part[:32].astype(f32) for part in parts]
    near, far = parts[0] + parts[1], parts[2] + parts[3]
    scale_near = lax.rsqrt(column(near[:, feats:], 0) / group_width + epsilon)
    scale_far = lax.rsqrt(column(far[:, feats:], 0) / group_width + epsilon)
    near, far = near[:, :feats] * scale_near, far[:, :feats] * scale_far
    summed = near + far
    summed = cat([summed[:8] + resid.astype(f32), summed[8:]]).astype(bf16)
    parts = around(cat([summed, cotangent]), "tok")
    cot_tok = cat([part[32:] for part in parts])
    stream = lax.reduce_precision(total([turned(parts[d][:32], d) for d in range(4)]), 8, 7)
    parts = around(cat([stream.astype(bf16), cot_tok, columns(scale_near, scale_far)], axis=1), "x")
    rows = cat(parts)
    far_rows = swapped(rows, "core", 1)
    group_scale = either(cat([rows[:, 2 * feats :], far_rows[:, 2 * feats :]]))
    mixed = (product_all.astype(f32) * group_scale).astype(bf16)

    width = w_up.shape[1]
    index = iy.astype(jnp.int32).reshape(1)
    outs = [(pltpu.VMEM, (64, width), f32)] + [(pltpu.VMEM, (64, width), bf16)] * 3
    outs += [(pltpu.VMEM, (64, width + AUX), f32)] + [(pltpu.VMEM, (64, width + AUX), bf16)] * 3
    outs += [(jax.ShapeDtypeStruct, (256, feats), bf16)] * 2
    scratch = [(256, width), (256, width + AUX)]
    fronts = local(
        front_kernel, outs, scratch, index, rows, far_rows, mlp_gain[None, :], w_down, w_up
    )
    back, raw, (rows, cot) = fronts[:4], fronts[4:8], fronts[8:]
    rows_float = rows.astype(f32)
    back = total([back[0]] + sent(back, "y"))
    back = back + swapped(back.astype(bf16), "zh", 1).astype(f32)
    back = cat(around(back.astype(bf16), "y"))
    parts = sent(raw, "y")
    raw = total([raw[0]] + parts)
    raw, squares = raw[:, :width], column(raw[:, width:], 0)
    other = swapped(cat([raw.astype(bf16), columns(squares)], axis=1), "zh", 1)
    squares = squares + column(other[:, width:], 0)
    stream_scale = lax.rsqrt(squares / D + epsilon)
    pre = (raw + other[:, :width].astype(f32)) * stream_scale
    pre = around(cat([pre.astype(bf16), columns(stream_scale)], axis=1), "y")
    pre, back = lax.optimization_barrier((pre, back))
    outs = [(pltpu.VMEM, (128, 2 * feats + AUX), bf16), (pltpu.VMEM, (128, AUX), f32)]
    outs += [(jax.ShapeDtypeStruct, (256, width), bf16)] * 2
    outs += [(jax.ShapeDtypeStruct, (256, AUX), bf16)]
    packed, inner, squared, delta, scales = local(
        hidden_kernel, outs, [(256, AUX)], index, *pre, back, w_down, w_up
    )
    scales = column(scales, 0)

    def down_half(rows):
        return jnp.dot(rows, w_down, preferred_element_type=f32).astype(bf16)

    other = swapped(packed, "core", 1)
    other = other.astype(f32)
    up_back = contract_cols(delta[:128], w_up) + other[:, :feats]
    down = other[:, feats : 2 * feats]
    inner = columns(column(inner + other[:, 2 * feats :], 0))
    packed = cat([up_back.astype(bf16), inner], axis=1)
    packed, squared = lax.optimization_barrier((packed, squared))
    parts = [packed[:32]] + sent([packed[32 * d : 32 * d + 32] for d in range(4)], "x")
    down = (down_half(squared[:128]).astype(f32) + down).astype(bf16)
    grad_w_down = contract_rows(squared, cot).astype(bf16)
    mine = total(parts)
    mine = cat([mine[:, :feats].astype(bf16), columns(column(mine[:, feats:], 0))], axis=1)
    mine, grad_w_down = lax.optimization_barrier((mine, grad_w_down))
    parts = around(mine, "tok")
    mine = total([turned(parts[d], d) for d in range(4)])
    up_back, inner = mine[:, :feats], column(mine[:, feats:], 0)
    own_scale = scales[:32]
    unit = stream * own_scale
    unit_back = up_back * mlp_gain[None, :]
    grads = lax.reduce_precision(
        cot_tok.astype(f32) + own_scale * (unit_back - unit * (inner / D)), 8, 7
    )
    grad_resid = grads[:8].astype(bf16)
    dot_near = jnp.sum(grads * near, axis=1, keepdims=True)
    dot_far = jnp.sum(grads * far, axis=1, keepdims=True)
    gain_sum = lines(jnp.sum(up_back * unit, axis=0, keepdims=True), feats + AUX)
    packed = cat([grads.astype(bf16), columns(dot_near, dot_far)], axis=1)
    packed = cat([packed, gain_sum])
    packed, delta = lax.optimization_barrier((packed, delta))
    parts = around(packed, "x")
    up_in = (rows_float * scales * mlp_gain[None, :]).astype(bf16)
    grad_w_up = contract_rows(up_in, delta).astype(bf16)
    gain_sum = lines(total([line(part[32:, :feats]) for part in parts]), feats + AUX)
    packed = cat([part[:32] for part in parts] + [gain_sum])
    packed, grad_w_up = lax.optimization_barrier((packed, grad_w_up))
    other = swapped(packed, "core", 1)
    grad_mlp_gain = (line(gain_sum) + line(other[128:]))[0, :feats]
    packed = cat([packed[:128], other[:128]])
    grads, dots = packed[:, :feats], either(packed[:, feats:])

    mixed_back = contract_cols(grads, w_out)
    gain_sum = jnp.sum(mixed_back * mixed.astype(f32), axis=0, keepdims=True)
    gain_sum = lines(gain_sum, units + AUX)
    rows = cat([mixed_back.astype(bf16), columns(dots, group_scale)], axis=1)
    rows = jnp.dot(to_norm, rows, preferred_element_type=f32).astype(bf16)
    group_scale = column(rows[:32, units:], 1)
    parts = [cat([rows[64 * d : 64 * d + 64], gain_sum]) for d in range(4)]
    parts, down, mixed, grads = lax.optimization_barrier((parts, down, mixed, grads))
    parts = parts[:1] + sent(parts, "y")
    down = [down[:32]] + sent([down[32 * d : 32 * d + 32] for d in range(4)], "x")
    summed = total(parts)
    mixed_back, gain_sum = summed[:64], lines(summed[64:65] + summed[65:66], units + AUX)
    dots = column(mixed_back[:, units:], 0)
    down = jnp.where(dots[:32] == dots[:32], total(down), 0.0)
    packed = cat([mixed_back[32:, :units].astype(bf16), columns(dots[32:])], axis=1)
    packed = cat([packed, gain_sum])
    other = swapped(packed, "zh", 1)
    parts = [down[:8]] + sent([down[8 * d : 8 * d + 8].astype(bf16) for d in range(4)], "tok")
    parts, gain_other = lax.optimization_barrier((parts, other[32:]))
    block_out = (stream[:8] + total(parts)).astype(bf16)
    grad_w_out = contract_rows(mixed, grads).astype(bf16)
    mixed_back = mixed_back[:32, :units] + other[:32, :units].astype(f32)
    dots = dots[:32] + column(other[:32, units:], 0)
    grad_norm_gain = (line(gain_sum) + line(gain_other))[0, :units] / norm_gain
    normed = product * group_scale
    product_back = group_scale * (mixed_back * norm_gain[None, :] - normed * (dots / group_width))
    grad_scan = (product_back * gated_unit).astype(bf16)
    grad_gate = (
        product_back * scan_float * logistic * (1.0 + gate_float * (1.0 - logistic))
    ).astype(bf16)
    return (
        block_out,
        grad_scan,
        grad_gate,
        grad_norm_gain,
        grad_w_out,
        grad_resid,
        grad_mlp_gain,
        grad_w_up,
        grad_w_down,
    )


def solution(mesh):
    fine = Mesh(mesh.devices.reshape(4, 4, 2, 4, 2), ("tok", "x", "core", "y", "zh"))
    tk, nout = ("tok", "x", "core"), ("y", "zh")
    in_specs = (
        P(nout, tk),
        P(nout, tk),
        P(tk),
        P(tk, nout),
        P(tk, nout),
        P(nout),
        P(nout, tk),
        P(tk, nout),
        P(tk, nout),
    )
    out_specs = (
        P(tk, nout),
        P(nout, tk),
        P(nout, tk),
        P(tk),
        P(tk, nout),
        P(tk, nout),
        P(nout),
        P(nout, tk),
        P(tk, nout),
    )
    return jax.shard_map(shards, mesh=fine, in_specs=in_specs, out_specs=out_specs, check_vma=False)
```
